512 devices in a mesh: seq: 32 (over y, x, core), grp: 16 (over z).
Axes of the slice: x: 4, y: 4, z: 16, core: 2. Of those that a mesh axis runs over, the one named last changes fastest.
Arguments:
- query: bfloat16 [16, 32, 4, 24, 4096], P('grp', 'seq'), may hold values from -6 to 6
- key_states: bfloat16 [16, 32, 4, 24, 4096], P('grp', 'seq'), may hold values from -6 to 6
- value_states: bfloat16 [16, 32, 4, 24, 4096], P('grp', 'seq'), may hold values from -12 to 12
- latent: float32 [16, 32, 4, 24, 64], P('grp', 'seq'), may hold values from -6 to 6
- sigma: float32 [16], P('grp'), may hold values from 0.3 to 1
- head_weight: bfloat16 [4096, 64], replicated, may hold values from -0.09375 to 0.09375
- latent_scale: float32 [16], replicated, may hold values from 0.5 to 2
- latent_shift: float32 [16], replicated, may hold values from -2 to 2
- frame_tail: bfloat16 [16, 2, 64, 48, 16], P(None, None, 'seq', 'grp'), may hold values from -6 to 6
- conv_weight: bfloat16 [432, 384], replicated, may hold values from -0.3125 to 0.3125
- conv_bias: float32 [384], replicated, may hold values from -4 to 4
Outputs:
- decoded: bfloat16 [16, 4, 64, 48, 384], P(None, None, 'seq', 'grp')
The draws below stay inside these ranges and needn't reach their ends.
All inputs are finite; a program needn't handle non-finite values.
Results may differ from the reference program's by a relative error of at most 0.011.
Values may be sent and summed in bfloat16 or wider, within the bound.
No kernel may reach another device: no remote copies, remote signals or barrier semaphores. Data moves between devices by JAX's collectives and lax.ppermute only.
A program may use at most 64 MiB of HBM per device.

```python
import math
import jax
import jax.numpy as jnp
from jax import lax

FR = 4
TC = 24
HEADS = 32
HD = 128
LAT_CH = 16
CONV_CH = 384
TAIL = 2
SAMPLES = 16
TR = 32
SEQ_LEN = 3072
PATCH_CH = 64
LR = 64
LC = 48


def draw_query(key, part):
    key = jax.random.fold_in(key, 3)
    full_shape = (SAMPLES, TR, FR, TC, HEADS * HD)
    drawn = jnp.clip(jax.random.normal(key, full_shape, jnp.float32), -6.0, 6.0)
    return drawn.astype(jnp.bfloat16)


def draw_key_states(key, part):
    key = jax.random.fold_in(key, 5)
    full_shape = (SAMPLES, TR, FR, TC, HEADS * HD)
    drawn = jnp.clip(jax.random.normal(key, full_shape, jnp.float32), -6.0, 6.0)
    return drawn.astype(jnp.bfloat16)


def draw_value_states(key, part):
    key = jax.random.fold_in(key, 7)
    full_shape = (SAMPLES, TR, FR, TC, HEADS * HD)
    channel = lax.broadcasted_iota(jnp.int32, full_shape, 4)
    head_index = (channel // HD).astype(jnp.float32)
    rising = 1.0 + 2.0 * head_index / max(HEADS - 1, 1)
    drawn = jnp.clip(jax.random.normal(key, full_shape, jnp.float32), -4.0, 4.0) * rising
    return drawn.astype(jnp.bfloat16)


def block_levels(stream_key, dims, cuts, low, largest):
    gain, own = 1.0, jax.random.fold_in(stream_key, 6)
    for axis_at, parts in cuts:
        heights = jnp.exp(jax.random.uniform(jax.random.fold_in(own, axis_at), (parts,), jnp.float32, low / len(cuts), largest / len(cuts)))
        gain = gain * jnp.repeat(heights, dims[axis_at] // parts).reshape([-1 if axis == axis_at else 1 for axis in range(len(dims))])
    return gain


def normal_values(own_key, extent, width, reach, cuts=(), kind=jnp.bfloat16):
    loudness = block_levels(own_key, extent, cuts, -0.22, 0.18) if cuts else 1.0
    result = jax.random.normal(own_key, extent, jnp.float32) * width * loudness
    return jnp.minimum(jnp.maximum(result, -reach), reach).astype(kind)


def setup_inputs(seed: int = 0) -> dict:
    keys = jax.random.split(jax.random.key(seed), 12)
    query = draw_query(jax.random.fold_in(keys[11], 71), 0)
    key_states = draw_key_states(jax.random.fold_in(keys[11], 71), 0)
    value_states = draw_value_states(jax.random.fold_in(keys[11], 71), 0)
    latent = normal_values(keys[3], (SAMPLES, TR, FR, TC, PATCH_CH), 1.0, 6.0, ((0, 16), (1, 32)), jnp.float32)
    sigma = jnp.clip(0.3 + 0.7 * jax.random.uniform(keys[4], (SAMPLES,), jnp.float32) ** block_levels(keys[4], (SAMPLES,), ((0, 16),), -0.2, 0.2), 0.3, 1.0)
    head_weight = normal_values(keys[5], (HEADS * HD, PATCH_CH), (HEADS * HD) ** -0.5, 0.09375)
    latent_scale = jnp.clip(jnp.exp(jax.random.uniform(keys[6], (LAT_CH,), jnp.float32, math.log(0.5), math.log(2.0))), 0.5, 2.0)
    latent_shift = normal_values(keys[7], (LAT_CH,), 0.5, 2.0, (), jnp.float32)
    frame_tail = normal_values(keys[8], (SAMPLES, TAIL, LR, LC, LAT_CH), 1.0, 6.0, ((2, 32), (3, 16)))
    conv_weight = normal_values(keys[9], (27 * LAT_CH, CONV_CH), (27 * LAT_CH) ** -0.5, 0.3125)
    conv_bias = normal_values(keys[10], (CONV_CH,), 1.0, 4.0, (), jnp.float32)
    return dict(query=query, key_states=key_states, value_states=value_states, latent=latent, sigma=sigma, head_weight=head_weight, latent_scale=latent_scale, latent_shift=latent_shift, frame_tail=frame_tail, conv_weight=conv_weight, conv_bias=conv_bias)


norm_eps = 1e-06

def head_attention(operands):
    queries, keys_here, values_here = operands
    scores = jnp.dot(queries, keys_here.T, preferred_element_type=jnp.float32) * (1.0 / math.sqrt(HD))
    peak = lax.optimization_barrier(jnp.max(scores, axis=1, keepdims=True))
    exponent_vals = jnp.exp(scores - peak)
    totals = lax.optimization_barrier(jnp.sum(exponent_vals, axis=1, keepdims=True))
    weights = exponent_vals.astype(jnp.bfloat16)
    mixed = jnp.dot(weights, values_here, preferred_element_type=jnp.float32) / totals
    return mixed.astype(jnp.bfloat16)

def conv_taps(padded, frame_count, row_count, col_count):
    pieces = []
    for time_off in range(3):
        for row_off in range(3):
            for col_off in range(3):
                pieces.append(padded[:, time_off:time_off + frame_count, row_off:row_off + row_count, col_off:col_off + col_count, :])
    return jnp.concatenate(pieces, axis=-1)

def decode_block(padded, conv_weight, conv_bias, frame_count, row_count, col_count):
    stacked = conv_taps(padded, frame_count, row_count, col_count)
    leading = stacked.shape[:-1]
    conv_out = jnp.dot(stacked.reshape(-1, stacked.shape[-1]), conv_weight, preferred_element_type=jnp.float32) + conv_bias
    normed = conv_out / jnp.sqrt(lax.optimization_barrier(jnp.mean(conv_out * conv_out, axis=1, keepdims=True)) + norm_eps)
    return jax.nn.silu(normed).astype(jnp.bfloat16).reshape(leading + (conv_weight.shape[1],))

def by_head(array):
    return array.reshape(SAMPLES, SEQ_LEN, HEADS, HD).transpose(0, 2, 1, 3).reshape(SAMPLES * HEADS, SEQ_LEN, HD)

def reference(query, key_states, value_states, latent, sigma, head_weight, latent_scale, latent_shift, frame_tail, conv_weight, conv_bias):
    attended = lax.map(head_attention, (by_head(query), by_head(key_states), by_head(value_states)))
    attended = attended.reshape(SAMPLES, HEADS, SEQ_LEN, HD).transpose(0, 2, 1, 3).reshape(SAMPLES * SEQ_LEN, HEADS * HD)
    widened = attended.astype(jnp.float32)
    mean_sq = lax.optimization_barrier(jnp.mean(widened * widened, axis=1, keepdims=True))
    projected = jnp.dot(attended, head_weight, preferred_element_type=jnp.float32)
    velocity = projected / jnp.sqrt(mean_sq + norm_eps)
    noise_level = jnp.repeat(sigma, SEQ_LEN)[:, None]
    cleaned = latent.reshape(SAMPLES * SEQ_LEN, PATCH_CH) - noise_level * velocity
    scaled = (cleaned.reshape(-1, 4, LAT_CH) * latent_scale + latent_shift).astype(jnp.bfloat16)
    image = scaled.reshape(SAMPLES, TR, FR, TC, 2, 2, LAT_CH).transpose(0, 2, 1, 4, 3, 5, 6).reshape(SAMPLES, FR, 2 * TR, 2 * TC, LAT_CH)
    window = jnp.concatenate([frame_tail, image], axis=1)
    padded = jnp.pad(window, ((0, 0), (0, 0), (1, 1), (1, 1), (0, 0)))
    return decode_block(padded, conv_weight, conv_bias, FR, 2 * TR, 2 * TC)
```

```python
import functools
import math

import jax
import jax.numpy as jnp
import numpy as np
from jax import lax
from jax.experimental import pallas as pl
from jax.experimental.pallas import tpu as pltpu
from jax.sharding import PartitionSpec as P

HD = 128
LAT_CH = 16
NORM_EPS = 1e-06
F32 = jnp.float32
BF16 = jnp.bfloat16
VMEM = pltpu.VMEM
SIDE = 2 * LAT_CH


def dot_nt(a, b):
    return lax.dot_general(a, b, (((1,), (1,)), ((), ())), preferred_element_type=F32)


def dot_nn(a, b):
    return jnp.dot(a, b, preferred_element_type=F32)


def pack_kernel(q_ref, k_ref, v_ref, o_ref):
    rows = q_ref.shape[0]
    for place, ref in enumerate((q_ref, k_ref, v_ref)):
        for head in range(o_ref.shape[0]):
            o_ref[head, place * rows : (place + 1) * rows, :] = ref[:, head * HD : (head + 1) * HD]


def pack_heads(query, keys, values, heads, steps=4):
    rows, features = query.shape
    width = features // steps
    spec = pl.BlockSpec((rows, width), lambda i: (0, i))
    return pl.pallas_call(
        pack_kernel,
        grid=(steps,),
        in_specs=[spec] * 3,
        out_specs=pl.BlockSpec((heads // steps, 3 * rows, HD), lambda i: (i, 0, 0)),
        out_shape=jax.ShapeDtypeStruct((heads, 3 * rows, HD), BF16),
        name="pack_heads",
    )(query, keys, values)


def attend_kernel(block_tr, x_ref, w_ref, o_ref, kt, vx, s_even, s_odd, mx_even, mx_odd, vel, ssq):
    tr, rows3, _ = x_ref.shape
    rows = rows3 // 3
    tokens = tr * rows
    block = block_tr * rows
    steps = tr // block_tr
    factor = math.log2(math.e) / math.sqrt(HD)
    for r in range(tr):
        at = slice(r * rows, (r + 1) * rows)
        vx[at, :HD] = x_ref[r, 2 * rows :, :]
        vx[at, HD:] = jnp.ones((rows, HD), BF16)
    for c in range(0, tr, 4):
        keys = x_ref[c : c + 4, rows : 2 * rows, :].reshape(4 * rows, HD)
        flipped = keys.astype(F32).T.astype(BF16)
        at = slice(c * rows, (c + 4) * rows)
        kt[:HD, at] = flipped
        kt[HD:, at] = flipped
    ssq[...] = jnp.zeros_like(ssq)

    chunk = 512

    def score(step, s_ref, mx_ref):
        q = x_ref[pl.ds(step * block_tr, block_tr), :rows, :].reshape(block, HD)
        q = q.astype(F32) * factor
        high = q.astype(BF16)
        low = (q - high.astype(F32)).astype(BF16)
        both = jnp.concatenate([high, low], axis=1)
        peak = None
        for c in range(0, tokens, chunk):
            s = dot_nn(both, kt[:, c : c + chunk])
            s_ref[:, c : c + chunk] = s
            for l in range(0, chunk, HD):
                part = s[:, l : l + HD]
                peak = part if peak is None else jnp.maximum(peak, part)
        mx_ref[...] = jnp.broadcast_to(jnp.max(peak, axis=1, keepdims=True), mx_ref.shape)

    def mix(step, s_ref, mx_ref):
        peak = mx_ref[...]
        weights = jnp.concatenate(
            [
                jnp.exp2(s_ref[:, l : l + HD] - peak).astype(BF16)
                for l in range(0, tokens, HD)
            ],
            axis=1,
        )
        mixed = dot_nn(weights, vx[...])
        att = (mixed[:, :HD] / mixed[:, HD:]).astype(BF16)
        vel[pl.ds(pl.multiple_of(step * block, block), block), :] = dot_nn(att, w_ref[...])
        wide = att.astype(F32)
        squares = (wide * wide).astype(BF16)
        ones = jnp.ones((16, HD), BF16)
        for r in range(block_tr):
            total = dot_nt(ones, squares[r * rows : (r + 1) * rows, :])
            ssq[step * block_tr + r, :, :rows] = total

    score(0, s_even, mx_even)

    @pl.loop(0, steps // 2 - 1)
    def _(i):
        score(2 * i + 1, s_odd, mx_odd)
        mix(2 * i, s_even, mx_even)
        score(2 * i + 2, s_even, mx_even)
        mix(2 * i + 1, s_odd, mx_odd)

    score(steps - 1, s_odd, mx_odd)
    mix(steps - 2, s_even, mx_even)
    mix(steps - 1, s_odd, mx_odd)

    lane = lax.broadcasted_iota(jnp.int32, (rows, HD), 1)
    line = lax.broadcasted_iota(jnp.int32, (16, HD), 0)
    for r in range(tr):
        up, down = (r - 1) % tr, (r + 1) % tr
        piece = [vel[t * rows : (t + 1) * rows, :] for t in (up, r, down)]
        merged = jnp.where(lane < SIDE, piece[0], jnp.where(lane < 3 * SIDE, piece[1], piece[2]))
        o_ref[r, :rows, :] = merged.astype(BF16)
        merged = jnp.where(line == 0, ssq[up], jnp.where(line == 1, ssq[r], ssq[down]))
        o_ref[r, rows:, :] = merged.astype(BF16)


def attend(x, w, block_tr=4):
    tr, rows3, _ = x.shape
    rows = rows3 // 3
    tokens, block = tr * rows, block_tr * rows
    return pl.pallas_call(
        functools.partial(attend_kernel, block_tr),
        in_specs=[pl.BlockSpec(memory_space=VMEM)] * 2,
        out_specs=pl.BlockSpec(memory_space=VMEM),
        out_shape=jax.ShapeDtypeStruct((tr, rows + 16, HD), BF16),
        scratch_shapes=[
            VMEM((2 * HD, tokens), BF16),
            VMEM((tokens, 2 * HD), BF16),
            VMEM((block, tokens), F32),
            VMEM((block, tokens), F32),
            VMEM((block, HD), F32),
            VMEM((block, HD), F32),
            VMEM((tokens, HD), F32),
            VMEM((tr, 16, HD), F32),
        ],
        compiler_params=pltpu.CompilerParams(vmem_limit_bytes=48 << 20),
        cost_estimate=pl.CostEstimate(
            flops=8 * tokens * tokens * HD, bytes_accessed=4 << 20, transcendentals=tokens * tokens
        ),
        name="attend",
    )(x, w)


def update_kernel(features, bands, index_ref, sigma_ref, y_ref, lat_ref, gain_ref, shift_ref, o_ref):
    heads, lines, _ = y_ref.shape
    rows = lines - 16
    frames = 4
    cols = rows // frames
    total = y_ref[0].astype(F32)
    for h in range(1, heads):
        total = total + y_ref[h].astype(F32)
    velocity = total[:rows]
    sums = jnp.concatenate([total[rows:], jnp.zeros((HD - 16, HD), F32)], axis=0).T
    lane = lax.broadcasted_iota(jnp.int32, (rows, HD), 1)
    up, own, down = (jnp.broadcast_to(sums[:rows, i : i + 1], (rows, HD)) for i in range(3))
    square = jnp.where(lane < SIDE, up, jnp.where(lane < 3 * SIDE, own, down))
    velocity = velocity / jnp.sqrt(square * (1.0 / features) + NORM_EPS)
    cleaned = lat_ref[...] - sigma_ref[0] * velocity
    scaled = cleaned * gain_ref[...] + shift_ref[...]
    first, last = index_ref[0] == 0, index_ref[0] == heads - 1
    drop = ((lane < SIDE) & first) | ((lane >= 3 * SIDE) & last)
    scaled = jnp.where(drop, 0.0, scaled).astype(BF16)
    count = bands * 4 * frames
    at = lax.broadcasted_iota(jnp.int32, (count, rows), 0)
    source = lax.broadcasted_iota(jnp.int32, (count, rows), 1)
    band, frame, t = at // (4 * frames), (at // 4) % frames, at % 4
    column = (3 * band + 1) // 2 - 1 + t
    hit = (source == frame * cols + column) & (column >= 0) & (column < cols)
    chosen = jnp.where(hit, 1.0, 0.0).astype(BF16)
    o_ref[...] = dot_nn(chosen, scaled).astype(BF16).reshape(o_ref.shape)


def update(index, sigma, y, lat, gain, shift, features, bands):
    smem = pl.BlockSpec(memory_space=pltpu.SMEM)
    vmem = pl.BlockSpec(memory_space=VMEM)
    return pl.pallas_call(
        functools.partial(update_kernel, features, bands),
        in_specs=[smem, smem] + [vmem] * 4,
        out_specs=vmem,
        out_shape=jax.ShapeDtypeStruct((bands, 16, HD), BF16),
        compiler_params=pltpu.CompilerParams(vmem_limit_bytes=16 << 20),
        name="update",
    )(index, sigma, y, lat, gain, shift)


STARTS = (((0, 1), (1, 0), (1, 1)), ((0, 0), (0, 1), (1, 0)))


def taps_kernel(w_ref, o_ref):
    out = w_ref.shape[1]
    o_ref[...] = jnp.zeros_like(o_ref)
    for kind, start in enumerate(STARTS):
        for tf in range(3):
            for ti in range(3):
                for tj, (token, b) in enumerate(start):
                    tap = ((tf * 3 + ti) * 3 + tj) * LAT_CH
                    piece = w_ref[tap : tap + LAT_CH, :]
                    for i in range(2):
                        at = tf * 2 * HD + token * HD + (i + ti) * SIDE + b * LAT_CH
                        o_ref[kind, at : at + LAT_CH, i * out : (i + 1) * out] = piece


def spread_taps(conv_weight):
    out = conv_weight.shape[1]
    return pl.pallas_call(
        taps_kernel,
        in_specs=[pl.BlockSpec(memory_space=VMEM)],
        out_specs=pl.BlockSpec(memory_space=VMEM),
        out_shape=jax.ShapeDtypeStruct((2, 6 * HD, 2 * out), BF16),
        compiler_params=pltpu.CompilerParams(vmem_limit_bytes=16 << 20),
        name="spread_taps",
    )(conv_weight)


def conv_kernel(index_ref, z_ref, cached_ref, taps_ref, bias_ref, o_ref):
    videos, lines, _ = z_ref.shape
    frames = lines // 4
    out = bias_ref.shape[1]
    odd = index_ref[0] % 2
    count = videos * frames
    at = lax.broadcasted_iota(jnp.int32, (3 * count, videos * lines), 0)
    source = lax.broadcasted_iota(jnp.int32, (3 * count, videos * lines), 1)
    t, frame, video = at // count, (at // videos) % frames, at % videos
    chosen = jnp.where(source == video * lines + frame * 4 + t, 1.0, 0.0).astype(BF16)
    image = dot_nn(chosen, z_ref[...].reshape(videos * lines, HD)).astype(BF16)
    token = [
        jnp.concatenate([cached_ref[t], image[t * count : (t + 1) * count]], axis=0)
        for t in range(3)
    ]

    def windows(first, second):
        wide = jnp.concatenate([first, second], axis=1)
        return jnp.concatenate([wide[tf * videos : tf * videos + count] for tf in range(3)], axis=1)

    middle = jnp.where(odd == 1, windows(token[0], token[1]), windows(token[1], token[2]))
    outer = jnp.concatenate([windows(token[0], token[1]), windows(token[1], token[2])], axis=0)
    outer = dot_nn(outer, taps_ref[odd])
    inner = dot_nn(middle, taps_ref[1 - odd])
    for i in range(2):
        done = []
        for part in (outer[:count], inner, outer[count:]):
            conv = part[:, i * out : (i + 1) * out] + bias_ref[...]
            mean_sq = jnp.mean(conv * conv, axis=1, keepdims=True)
            normed = conv / jnp.sqrt(mean_sq + NORM_EPS)
            done.append(normed / (1.0 + jnp.exp(-normed)))
        for f in range(frames):
            at = slice(f * videos, (f + 1) * videos)
            tile = jnp.concatenate([d[at][:, None, :] for d in done], axis=1)
            o_ref[:, f, i] = tile.astype(BF16)


def convolve(index, z, cached, taps, bias):
    videos, lines, _ = z.shape
    out = bias.shape[1]
    vmem = pl.BlockSpec(memory_space=VMEM)
    return pl.pallas_call(
        conv_kernel,
        in_specs=[pl.BlockSpec(memory_space=pltpu.SMEM)] + [vmem] * 4,
        out_specs=vmem,
        out_shape=jax.ShapeDtypeStruct((videos, lines // 4, 2, 3, out), BF16),
        compiler_params=pltpu.CompilerParams(vmem_limit_bytes=32 << 20),
        name="convolve",
    )(index, z, cached, taps, bias)


def neighbours(head, tail, axis):
    count = lax.axis_size(axis)
    before = lax.ppermute(tail, axis, [(i, i + 1) for i in range(count - 1)])
    after = lax.ppermute(head, axis, [(i + 1, i) for i in range(count - 1)])
    return before, after


def on_device(
    query,
    key_states,
    value_states,
    latent,
    sigma,
    head_weight,
    latent_scale,
    latent_shift,
    frame_tail,
    conv_weight,
    conv_bias,
):
    features = query.shape[4]
    heads = features // HD
    frames, cols = latent.shape[2], latent.shape[3]
    rows = frames * cols
    bands = lax.axis_size("grp")
    seq_at, grp_at = lax.axis_index("seq"), lax.axis_index("grp")
    videos, tail_frames = frame_tail.shape[0], frame_tail.shape[1]

    sent = pack_heads(
        query.reshape(rows, features),
        key_states.reshape(rows, features),
        value_states.reshape(rows, features),
        heads,
    )
    mine = lax.all_to_all(sent, "seq", 0, 0, tiled=True)

    lat = latent.reshape(rows, 4 * LAT_CH)
    cached = jnp.transpose(frame_tail, (0, 1, 3, 2, 4))
    flat = (videos * tail_frames * frame_tail.shape[3] * LAT_CH // SIDE, SIDE)
    top = jnp.concatenate([lat[:, :SIDE], cached[:, :, :, 0].astype(F32).reshape(flat)], axis=0)
    low = jnp.concatenate([lat[:, SIDE:], cached[:, :, :, -1].astype(F32).reshape(flat)], axis=0)
    above, below = neighbours(top, low, "seq")
    lat = jnp.concatenate([above[:rows], lat, below[:rows]], axis=1)
    above, below = (
        side[rows:].astype(BF16).reshape(cached[:, :, :, :1].shape) for side in (above, below)
    )
    cached = jnp.concatenate([above, cached, below], axis=3)
    left, right = neighbours(cached[:, :, :1], cached[:, :, -1:], "grp")
    cached = jnp.concatenate([left, cached, right], axis=2)
    none = jnp.zeros_like(left)
    cached = jnp.where(
        grp_at % 2 == 0,
        jnp.concatenate([none, cached], axis=2),
        jnp.concatenate([cached, none], axis=2),
    )
    cached = cached.reshape(videos, tail_frames, 3, 2, 4, LAT_CH).transpose(2, 1, 0, 4, 3, 5)
    cached = cached.reshape(3, tail_frames * videos, HD)

    taps = spread_taps(conv_weight)
    w = lax.dynamic_slice_in_dim(head_weight, seq_at * HD, HD, axis=0)
    w = jnp.concatenate([w[:, SIDE:], w, w[:, :SIDE]], axis=1)
    gain = jnp.tile(latent_scale, HD // LAT_CH).reshape(1, HD)
    shift = jnp.tile(latent_shift, HD // LAT_CH).reshape(1, HD)

    parts = lax.all_to_all(attend(mine, w), "seq", 0, 0, tiled=True)
    bands_out = update(seq_at.reshape(1), sigma, parts, lat, gain, shift, features, bands)
    tiles = lax.all_to_all(bands_out, "grp", 0, 0, tiled=True)
    return convolve(grp_at.reshape(1), tiles, cached, taps, conv_bias.reshape(1, -1))


def solution(mesh):
    return jax.shard_map(
        on_device,
        mesh=mesh,
        in_specs=(
            P("grp", "seq", None, None, None),
            P("grp", "seq", None, None, None),
            P("grp", "seq", None, None, None),
            P("grp", "seq", None, None, None),
            P("grp"),
            P(),
            P(),
            P(),
            P(None, None, "seq", "grp", None),
            P(),
            P(),
        ),
        out_specs=P(None, None, "seq", "grp", None),
        check_vma=False,
    )
```

```python
import functools
import math

import jax
import jax.numpy as jnp
import numpy as np
from jax import lax
from jax.experimental import pallas as pl
from jax.experimental.pallas import tpu as pltpu
from jax.sharding import PartitionSpec as P

HD = 128
LAT_CH = 16
NORM_EPS = 1e-06
F32 = jnp.float32
BF16 = jnp.bfloat16
VMEM = pltpu.VMEM
SIDE = 2 * LAT_CH


def dot_nt(a, b):
    return lax.dot_general(a, b, (((1,), (1,)), ((), ())), preferred_element_type=F32)


def dot_nn(a, b):
    return jnp.dot(a, b, preferred_element_type=F32)


def pack_kernel(q_ref, k_ref, v_ref, o_ref):
    rows = q_ref.shape[0]
    for place, ref in enumerate((q_ref, k_ref, v_ref)):
        for head in range(o_ref.shape[0]):
            o_ref[head, place * rows : (place + 1) * rows, :] = ref[:, head * HD : (head + 1) * HD]


def pack_heads(query, keys, values, heads, steps=2):
    rows, features = query.shape
    width = features // steps
    spec = pl.BlockSpec((rows, width), lambda i: (0, i))
    return pl.pallas_call(
        pack_kernel,
        grid=(steps,),
        in_specs=[spec] * 3,
        out_specs=pl.BlockSpec((heads // steps, 3 * rows, HD), lambda i: (i, 0, 0)),
        out_shape=jax.ShapeDtypeStruct((heads, 3 * rows, HD), BF16),
        name="pack_heads",
    )(query, keys, values)


def attend_kernel(block, x_ref, w_ref, o_ref, qq, kk, vx, att, ssq, *buffers):
    tr, rows3, _ = x_ref.shape
    rows = rows3 // 3
    tokens = tr * rows
    steps = tokens // block
    factor = math.log2(math.e) / math.sqrt(HD)
    for r in range(tr):
        at = slice(r * rows, (r + 1) * rows)
        q = x_ref[r, :rows, :].astype(F32) * factor
        high = q.astype(BF16)
        qq[at, :HD] = high
        qq[at, HD:] = (q - high.astype(F32)).astype(BF16)
        vx[at, :HD] = x_ref[r, 2 * rows :, :]
        vx[at, HD:] = jnp.ones((rows, HD), BF16)
    for c in range(0, tr, 4):
        keys = x_ref[c : c + 4, rows : 2 * rows, :].reshape(4 * rows, HD)
        flipped = keys.astype(F32).T.astype(BF16)
        at = slice(c * rows, (c + 4) * rows)
        kk[:HD, at] = flipped
        kk[HD:, at] = flipped

    chunk = 512

    def score(step):
        s_ref, peak_ref = buffers[step % 2], buffers[2 + step % 2]
        q = qq[step * block : (step + 1) * block, :]
        peak = None
        for c in range(0, tokens, chunk):
            s = dot_nn(q, kk[:, c : c + chunk])
            s_ref[:, c : c + chunk] = s
            for l in range(0, chunk, HD):
                part = s[:, l : l + HD]
                peak = part if peak is None else jnp.maximum(peak, part)
        peak_ref[...] = jnp.broadcast_to(jnp.max(peak, axis=1, keepdims=True), peak_ref.shape)

    def mix(step):
        s_ref, peak_ref = buffers[step % 2], buffers[2 + step % 2]
        peak = peak_ref[...]
        weights = jnp.concatenate(
            [
                jnp.exp2(s_ref[:, l : l + HD] - peak).astype(BF16)
                for l in range(0, tokens, HD)
            ],
            axis=1,
        )
        mixed = dot_nn(weights, vx[...])
        att[step * block : (step + 1) * block, :] = (mixed[:, :HD] / mixed[:, HD:]).astype(BF16)

    score(0)
    for step in range(1, steps):
        score(step)
        mix(step - 1)
    mix(steps - 1)

    ssq[...] = jnp.zeros_like(ssq)
    ones = jnp.ones((16, HD), BF16)
    velocity = dot_nn(att[...], w_ref[...])
    for r in range(tr):
        wide = att[r * rows : (r + 1) * rows, :].astype(F32)
        ssq[r, :, :rows] = dot_nt(ones, (wide * wide).astype(BF16))
    lane = lax.broadcasted_iota(jnp.int32, (rows, HD), 1)
    line = lax.broadcasted_iota(jnp.int32, (16, HD), 0)
    for r in range(tr):
        up, down = (r - 1) % tr, (r + 1) % tr
        piece = [velocity[t * rows : (t + 1) * rows, :] for t in (up, r, down)]
        merged = jnp.where(lane < SIDE, piece[0], jnp.where(lane < 3 * SIDE, piece[1], piece[2]))
        o_ref[r, :rows, :] = merged.astype(BF16)
        merged = jnp.where(line == 0, ssq[up], jnp.where(line == 1, ssq[r], ssq[down]))
        o_ref[r, rows:, :] = merged.astype(BF16)


def attend(x, w, block=384):
    tr, rows3, _ = x.shape
    rows = rows3 // 3
    tokens = tr * rows
    return pl.pallas_call(
        functools.partial(attend_kernel, block),
        in_specs=[pl.BlockSpec(memory_space=VMEM)] * 2,
        out_specs=pl.BlockSpec(memory_space=VMEM),
        out_shape=jax.ShapeDtypeStruct((tr, rows + 16, HD), BF16),
        scratch_shapes=[
            VMEM((tokens, 2 * HD), BF16),
            VMEM((2 * HD, tokens), BF16),
            VMEM((tokens, 2 * HD), BF16),
            VMEM((tokens, HD), BF16),
            VMEM((tr, 16, HD), F32),
            VMEM((block, tokens), F32),
            VMEM((block, tokens), F32),
            VMEM((block, HD), F32),
            VMEM((block, HD), F32),
        ],
        compiler_params=pltpu.CompilerParams(vmem_limit_bytes=44 << 20),
        cost_estimate=pl.CostEstimate(
            flops=8 * tokens * tokens * HD, bytes_accessed=4 << 20, transcendentals=tokens * tokens
        ),
        name="attend",
    )(x, w)


def update_kernel(features, bands, index_ref, sigma_ref, y_ref, lat_ref, gain_ref, shift_ref, o_ref):
    heads, lines, _ = y_ref.shape
    rows = lines - 16
    frames = 4
    cols = rows // frames
    total = y_ref[0].astype(F32)
    for h in range(1, heads):
        total = total + y_ref[h].astype(F32)
    velocity = total[:rows]
    sums = jnp.concatenate([total[rows:], jnp.zeros((HD - 16, HD), F32)], axis=0).T
    lane = lax.broadcasted_iota(jnp.int32, (rows, HD), 1)
    up, own, down = (jnp.broadcast_to(sums[:rows, i : i + 1], (rows, HD)) for i in range(3))
    square = jnp.where(lane < SIDE, up, jnp.where(lane < 3 * SIDE, own, down))
    velocity = velocity / jnp.sqrt(square * (1.0 / features) + NORM_EPS)
    cleaned = lat_ref[...] - sigma_ref[0] * velocity
    scaled = cleaned * gain_ref[...] + shift_ref[...]
    first, last = index_ref[0] == 0, index_ref[0] == heads - 1
    drop = ((lane < SIDE) & first) | ((lane >= 3 * SIDE) & last)
    scaled = jnp.where(drop, 0.0, scaled).astype(BF16)
    count = bands * 4 * frames
    at = lax.broadcasted_iota(jnp.int32, (count, rows), 0)
    source = lax.broadcasted_iota(jnp.int32, (count, rows), 1)
    band, frame, t = at // (4 * frames), (at // 4) % frames, at % 4
    column = (3 * band + 1) // 2 - 1 + t
    hit = (source == frame * cols + column) & (column >= 0) & (column < cols)
    chosen = jnp.where(hit, 1.0, 0.0).astype(BF16)
    o_ref[...] = dot_nn(chosen, scaled).astype(BF16).reshape(o_ref.shape)


def update(index, sigma, y, lat, gain, shift, features, bands):
    smem = pl.BlockSpec(memory_space=pltpu.SMEM)
    vmem = pl.BlockSpec(memory_space=VMEM)
    return pl.pallas_call(
        functools.partial(update_kernel, features, bands),
        in_specs=[smem, smem] + [vmem] * 4,
        out_specs=vmem,
        out_shape=jax.ShapeDtypeStruct((bands, 16, HD), BF16),
        compiler_params=pltpu.CompilerParams(vmem_limit_bytes=16 << 20),
        name="update",
    )(index, sigma, y, lat, gain, shift)


STARTS = (((0, 1), (1, 0), (1, 1)), ((0, 0), (0, 1), (1, 0)))


def taps_kernel(w_ref, o_ref):
    out = w_ref.shape[1]
    o_ref[...] = jnp.zeros_like(o_ref)
    for kind, start in enumerate(STARTS):
        for tf in range(3):
            for ti in range(3):
                for tj, (token, b) in enumerate(start):
                    tap = ((tf * 3 + ti) * 3 + tj) * LAT_CH
                    piece = w_ref[tap : tap + LAT_CH, :]
                    for i in range(2):
                        at = tf * 2 * HD + token * HD + (i + ti) * SIDE + b * LAT_CH
                        o_ref[kind, at : at + LAT_CH, i * out : (i + 1) * out] = piece


def spread_taps(conv_weight):
    out = conv_weight.shape[1]
    return pl.pallas_call(
        taps_kernel,
        in_specs=[pl.BlockSpec(memory_space=VMEM)],
        out_specs=pl.BlockSpec(memory_space=VMEM),
        out_shape=jax.ShapeDtypeStruct((2, 6 * HD, 2 * out), BF16),
        compiler_params=pltpu.CompilerParams(vmem_limit_bytes=16 << 20),
        name="spread_taps",
    )(conv_weight)


def conv_kernel(index_ref, z_ref, cached_ref, taps_ref, bias_ref, o_ref):
    videos, lines, _ = z_ref.shape
    frames = lines // 4
    out = bias_ref.shape[1]
    odd = index_ref[0] % 2
    count = videos * frames
    at = lax.broadcasted_iota(jnp.int32, (3 * count, videos * lines), 0)
    source = lax.broadcasted_iota(jnp.int32, (3 * count, videos * lines), 1)
    t, frame, video = at // count, (at // videos) % frames, at % videos
    chosen = jnp.where(source == video * lines + frame * 4 + t, 1.0, 0.0).astype(BF16)
    image = dot_nn(chosen, z_ref[...].reshape(videos * lines, HD)).astype(BF16)
    token = [
        jnp.concatenate([cached_ref[t], image[t * count : (t + 1) * count]], axis=0)
        for t in range(3)
    ]

    def windows(first, second):
        wide = jnp.concatenate([first, second], axis=1)
        return jnp.concatenate([wide[tf * videos : tf * videos + count] for tf in range(3)], axis=1)

    middle = jnp.where(odd == 1, windows(token[0], token[1]), windows(token[1], token[2]))
    outer = jnp.concatenate([windows(token[0], token[1]), windows(token[1], token[2])], axis=0)
    outer = dot_nn(outer, taps_ref[odd])
    inner = dot_nn(middle, taps_ref[1 - odd])
    for j, part in enumerate((outer[:count], inner, outer[count:])):
        done = []
        for i in range(2):
            conv = part[:, i * out : (i + 1) * out] + bias_ref[...]
            mean_sq = jnp.mean(conv * conv, axis=1, keepdims=True)
            normed = conv / jnp.sqrt(mean_sq + NORM_EPS)
            done.append(normed / (1.0 + jnp.exp(-normed)))
        for f in range(frames):
            at = slice(f * videos, (f + 1) * videos)
            tile = jnp.concatenate([d[at][:, None, :] for d in done], axis=1)
            o_ref[:, f, j] = tile.astype(BF16)


def convolve(index, z, cached, taps, bias):
    videos, lines, _ = z.shape
    out = bias.shape[1]
    vmem = pl.BlockSpec(memory_space=VMEM)
    return pl.pallas_call(
        conv_kernel,
        in_specs=[pl.BlockSpec(memory_space=pltpu.SMEM)] + [vmem] * 4,
        out_specs=vmem,
        out_shape=jax.ShapeDtypeStruct((videos, lines // 4, 3, 2, out), BF16),
        compiler_params=pltpu.CompilerParams(vmem_limit_bytes=32 << 20),
        name="convolve",
    )(index, z, cached, taps, bias).transpose(0, 1, 3, 2, 4)


def neighbours(head, tail, axis):
    count = lax.axis_size(axis)
    before = lax.ppermute(tail, axis, [(i, i + 1) for i in range(count - 1)])
    after = lax.ppermute(head, axis, [(i + 1, i) for i in range(count - 1)])
    return before, after


def on_device(
    query,
    key_states,
    value_states,
    latent,
    sigma,
    head_weight,
    latent_scale,
    latent_shift,
    frame_tail,
    conv_weight,
    conv_bias,
):
    features = query.shape[4]
    heads = features // HD
    frames, cols = latent.shape[2], latent.shape[3]
    rows = frames * cols
    bands = lax.axis_size("grp")
    seq_at, grp_at = lax.axis_index("seq"), lax.axis_index("grp")
    videos, tail_frames = frame_tail.shape[0], frame_tail.shape[1]

    sent = pack_heads(
        query.reshape(rows, features),
        key_states.reshape(rows, features),
        value_states.reshape(rows, features),
        heads,
    )
    mine = lax.all_to_all(sent, "seq", 0, 0, tiled=True)

    lat = latent.reshape(rows, 4 * LAT_CH)
    cached = jnp.transpose(frame_tail, (0, 1, 3, 2, 4))
    flat = (videos * tail_frames * frame_tail.shape[3] * LAT_CH // SIDE, SIDE)
    top = jnp.concatenate([lat[:, :SIDE], cached[:, :, :, 0].astype(F32).reshape(flat)], axis=0)
    low = jnp.concatenate([lat[:, SIDE:], cached[:, :, :, -1].astype(F32).reshape(flat)], axis=0)
    above, below = neighbours(top, low, "seq")
    lat = jnp.concatenate([above[:rows], lat, below[:rows]], axis=1)
    above, below = (
        side[rows:].astype(BF16).reshape(cached[:, :, :, :1].shape) for side in (above, below)
    )
    cached = jnp.concatenate([above, cached, below], axis=3)
    left, right = neighbours(cached[:, :, :1], cached[:, :, -1:], "grp")
    cached = jnp.concatenate([left, cached, right], axis=2)
    none = jnp.zeros_like(left)
    cached = jnp.where(
        grp_at % 2 == 0,
        jnp.concatenate([none, cached], axis=2),
        jnp.concatenate([cached, none], axis=2),
    )
    cached = cached.reshape(videos, tail_frames, 3, 2, 4, LAT_CH).transpose(2, 1, 0, 4, 3, 5)
    cached = cached.reshape(3, tail_frames * videos, HD)

    taps = spread_taps(conv_weight)
    w = lax.dynamic_slice_in_dim(head_weight, seq_at * HD, HD, axis=0)
    w = jnp.concatenate([w[:, SIDE:], w, w[:, :SIDE]], axis=1)
    gain = jnp.tile(latent_scale, HD // LAT_CH).reshape(1, HD)
    shift = jnp.tile(latent_shift, HD // LAT_CH).reshape(1, HD)

    bias = conv_bias.reshape(1, -1)
    seq_at, grp_at = seq_at.reshape(1), grp_at.reshape(1)
    mine, w, lat, cached, taps, gain, shift, bias, sigma, seq_at, grp_at = lax.optimization_barrier(
        (mine, w, lat, cached, taps, gain, shift, bias, sigma, seq_at, grp_at)
    )

    parts = lax.all_to_all(attend(mine, w), "seq", 0, 0, tiled=True)
    bands_out = update(seq_at, sigma, parts, lat, gain, shift, features, bands)
    tiles = lax.all_to_all(bands_out, "grp", 0, 0, tiled=True)
    return convolve(grp_at, tiles, cached, taps, bias)


def solution(mesh):
    return jax.shard_map(
        on_device,
        mesh=mesh,
        in_specs=(
            P("grp", "seq", None, None, None),
            P("grp", "seq", None, None, None),
            P("grp", "seq", None, None, None),
            P("grp", "seq", None, None, None),
            P("grp"),
            P(),
            P(),
            P(),
            P(None, None, "seq", "grp", None),
            P(),
            P(),
        ),
        out_specs=P(None, None, "seq", "grp", None),
        check_vma=False,
    )
```

```python
import functools
import math

import jax
import jax.numpy as jnp
import numpy as np
from jax import lax
from jax.experimental import pallas as pl
from jax.experimental.pallas import tpu as pltpu
from jax.sharding import PartitionSpec as P

HD = 128
LAT_CH = 16
NORM_EPS = 1e-06
F32 = jnp.float32
BF16 = jnp.bfloat16
VMEM = pltpu.VMEM
SIDE = 2 * LAT_CH


def dot_nt(a, b):
    return lax.dot_general(a, b, (((1,), (1,)), ((), ())), preferred_element_type=F32)


def dot_nn(a, b):
    return jnp.dot(a, b, preferred_element_type=F32)


def pack_kernel(q_ref, k_ref, v_ref, o_ref):
    rows = q_ref.shape[0]
    for place, ref in enumerate((q_ref, k_ref, v_ref)):
        for head in range(o_ref.shape[0]):
            o_ref[head, place * rows : (place + 1) * rows, :] = ref[:, head * HD : (head + 1) * HD]


def pack_heads(query, keys, values, heads, steps=2):
    rows, features = query.shape
    width = features // steps
    spec = pl.BlockSpec((rows, width), lambda i: (0, i))
    return pl.pallas_call(
        pack_kernel,
        grid=(steps,),
        in_specs=[spec] * 3,
        out_specs=pl.BlockSpec((heads // steps, 3 * rows, HD), lambda i: (i, 0, 0)),
        out_shape=jax.ShapeDtypeStruct((heads, 3 * rows, HD), BF16),
        name="pack_heads",
    )(query, keys, values)


def attend_kernel(block_tr, x_ref, w_ref, o_ref, kk, vx, held, vel, ssq, msg, sem, *buffers):
    tr, rows3, _ = x_ref.shape
    rows = rows3 // 3
    tokens, block = tr * rows, block_tr * rows
    steps = tr // block_tr
    factor = math.log2(math.e) / math.sqrt(HD)
    chunk_tr = 8
    chunk = chunk_tr * rows

    def score(step):
        s_ref, peak_ref = buffers[step % 2], buffers[2 + step % 2]
        q = x_ref[step * block_tr : (step + 1) * block_tr, :rows, :].reshape(block, HD)
        q = q.astype(F32) * factor
        high = q.astype(BF16)
        q = jnp.concatenate([high, (q - high.astype(F32)).astype(BF16)], axis=1)
        peak = None
        for c in range(tr // chunk_tr):
            at = slice(c * chunk, (c + 1) * chunk)
            if step == 0:
                keys = x_ref[c * chunk_tr : (c + 1) * chunk_tr, rows : 2 * rows, :]
                flipped = keys.reshape(chunk, HD).astype(F32).T.astype(BF16)
                kk[:HD, at] = flipped
                kk[HD:, at] = flipped
            s = dot_nn(q, kk[:, at])
            s_ref[:, at] = s
            for l in range(0, chunk, HD):
                part = s[:, l : l + HD]
                peak = part if peak is None else jnp.maximum(peak, part)
        peak_ref[...] = jnp.broadcast_to(jnp.max(peak, axis=1, keepdims=True), peak_ref.shape)

    def mix(step):
        s_ref, peak_ref = buffers[step % 2], buffers[2 + step % 2]
        peak = peak_ref[...]
        weights = jnp.concatenate(
            [
                jnp.exp2(s_ref[:, l : l + HD] - peak).astype(BF16)
                for l in range(0, tokens, HD)
            ],
            axis=1,
        )
        mixed = dot_nn(weights, vx[...])
        held[step * block : (step + 1) * block, :] = (mixed[:, :HD] / mixed[:, HD:]).astype(BF16)

    lane = lax.broadcasted_iota(jnp.int32, (rows, HD), 1)
    line = lax.broadcasted_iota(jnp.int32, (16, HD), 0)

    def send(r):
        up, down = (r - 1) % tr, (r + 1) % tr
        piece = [vel[t * rows : (t + 1) * rows, :] for t in (up, r, down)]
        merged = jnp.where(lane < SIDE, piece[0], jnp.where(lane < 3 * SIDE, piece[1], piece[2]))
        msg[r, :rows, :] = merged.astype(BF16)
        merged = jnp.where(line == 0, ssq[up], jnp.where(line == 1, ssq[r], ssq[down]))
        msg[r, rows:, :] = merged.astype(BF16)
        pltpu.make_async_copy(msg.at[r], o_ref.at[r], sem).start()

    ssq[...] = jnp.zeros_like(ssq)
    score(0)
    for r in range(tr):
        at = slice(r * rows, (r + 1) * rows)
        vx[at, :HD] = x_ref[r, 2 * rows :, :]
        vx[at, HD:] = jnp.ones((rows, HD), BF16)
    for step in range(steps):
        if step + 1 < steps:
            score(step + 1)
        mix(step)
    vel[...] = dot_nn(held[...], w_ref[...])
    for r in range(tr):
        wide = held[r * rows : (r + 1) * rows, :].astype(F32)
        ssq[r, :, :rows] = dot_nt(jnp.ones((16, HD), BF16), (wide * wide).astype(BF16))
    for r in range(tr):
        send(r)
    pltpu.make_async_copy(msg, o_ref, sem).wait()


def attend(x, w, block_tr=4):
    tr, rows3, _ = x.shape
    rows = rows3 // 3
    tokens, block = tr * rows, block_tr * rows
    return pl.pallas_call(
        functools.partial(attend_kernel, block_tr),
        in_specs=[pl.BlockSpec(memory_space=VMEM)] * 2,
        out_specs=pl.BlockSpec(memory_space=pl.ANY),
        out_shape=jax.ShapeDtypeStruct((tr, rows + 16, HD), BF16),
        scratch_shapes=[
            VMEM((2 * HD, tokens), BF16),
            VMEM((tokens, 2 * HD), BF16),
            VMEM((tokens, HD), BF16),
            VMEM((tokens, HD), F32),
            VMEM((tr, 16, HD), F32),
            VMEM((tr, rows + 16, HD), BF16),
            pltpu.SemaphoreType.DMA,
            VMEM((block, tokens), F32),
            VMEM((block, tokens), F32),
            VMEM((block, HD), F32),
            VMEM((block, HD), F32),
        ],
        compiler_params=pltpu.CompilerParams(vmem_limit_bytes=44 << 20),
        cost_estimate=pl.CostEstimate(
            flops=8 * tokens * tokens * HD, bytes_accessed=4 << 20, transcendentals=tokens * tokens
        ),
        name="attend",
    )(x, w)


def update_kernel(
    features, bands, index_ref, sigma_ref, y_ref, lat_ref, above_ref, below_ref, gain_ref, shift_ref, o_ref
):
    heads, lines, _ = y_ref.shape
    rows = lines - 16
    frames = 4
    cols = rows // frames
    total = y_ref[0].astype(F32)
    for h in range(1, heads):
        total = total + y_ref[h].astype(F32)
    velocity = total[:rows]
    sums = jnp.concatenate([total[rows:], jnp.zeros((HD - 16, HD), F32)], axis=0).T
    lane = lax.broadcasted_iota(jnp.int32, (rows, HD), 1)
    up, own, down = (jnp.broadcast_to(sums[:rows, i : i + 1], (rows, HD)) for i in range(3))
    square = jnp.where(lane < SIDE, up, jnp.where(lane < 3 * SIDE, own, down))
    velocity = velocity / jnp.sqrt(square * (1.0 / features) + NORM_EPS)
    above = above_ref[above_ref.shape[0] - rows :, :].astype(F32)
    below = below_ref[below_ref.shape[0] - rows :, :].astype(F32)
    above = above + pltpu.roll(above, HD - SIDE, 1) + pltpu.roll(above, HD - 2 * SIDE, 1)
    below = pltpu.roll(below, 3 * SIDE, 1) + pltpu.roll(below, 2 * SIDE, 1) + pltpu.roll(below, SIDE, 1)
    lat = jnp.where(lane < SIDE, above, jnp.where(lane < 3 * SIDE, lat_ref[...], below))
    cleaned = lat - sigma_ref[0] * velocity
    scaled = cleaned * gain_ref[...] + shift_ref[...]
    first, last = index_ref[0] == 0, index_ref[0] == heads - 1
    drop = ((lane < SIDE) & first) | ((lane >= 3 * SIDE) & last)
    scaled = jnp.where(drop, 0.0, scaled).astype(BF16)
    count = bands * 4 * frames
    at = lax.broadcasted_iota(jnp.int32, (count, rows), 0)
    source = lax.broadcasted_iota(jnp.int32, (count, rows), 1)
    band, frame, t = at // (4 * frames), (at // 4) % frames, at % 4
    column = (3 * band + 1) // 2 - 1 + t
    hit = (source == frame * cols + column) & (column >= 0) & (column < cols)
    chosen = jnp.where(hit, 1.0, 0.0).astype(BF16)
    o_ref[...] = dot_nn(chosen, scaled).astype(BF16).reshape(o_ref.shape)


def update(index, sigma, y, lat, above, below, gain, shift, features, bands):
    smem = pl.BlockSpec(memory_space=pltpu.SMEM)
    vmem = pl.BlockSpec(memory_space=VMEM)
    return pl.pallas_call(
        functools.partial(update_kernel, features, bands),
        in_specs=[smem, smem] + [vmem] * 6,
        out_specs=vmem,
        out_shape=jax.ShapeDtypeStruct((bands, 16, HD), BF16),
        compiler_params=pltpu.CompilerParams(vmem_limit_bytes=16 << 20),
        name="update",
    )(index, sigma, y, lat, above, below, gain, shift)


AROUND = ((1, 0), (-1, 0), (0, 1), (0, -1), (1, 1), (1, -1), (-1, 1), (-1, -1))


def edges_kernel(index_ref, tail_ref, lat_ref, own_ref, *out_refs):
    count, width = tail_ref.shape
    odd = index_ref[0] % 2
    shape = (width, 3 * HD)
    k = lax.broadcasted_iota(jnp.int32, shape, 0)
    n = lax.broadcasted_iota(jnp.int32, shape, 1)
    pixel = k // LAT_CH
    i = jnp.where(pixel >= 3, 1, 0)
    j = pixel - 3 * i
    same = (k % LAT_CH) == (n % LAT_CH)
    slot = 2 * (n // HD) + (n % SIDE) // LAT_CH
    row = (n % HD) // SIDE
    for (dr, dz), out_ref in zip(((0, 0),) + AROUND, (own_ref,) + out_refs):
        shift = 1 - odd if dz == 0 else odd
        hit = same & (row == i + (1 - 2 * dr)) & (slot == j + (1 - 3 * dz) + shift)
        if dz:
            hit = hit & (j == (2 if dz == 1 else 0))
        placed = dot_nn(tail_ref[...], jnp.where(hit, 1.0, 0.0).astype(BF16)).astype(BF16)
        for t in range(3):
            out_ref[t * count : (t + 1) * count, :] = placed[:, t * HD : (t + 1) * HD]
    lat = lat_ref[...]
    high = lat.astype(BF16).astype(F32)
    rest = lat - high
    mid = rest.astype(BF16).astype(F32)
    low = rest - mid
    lane = lax.broadcasted_iota(jnp.int32, lat.shape, 1)
    for out_ref, start in zip(out_refs[:2], (2 * SIDE, SIDE)):
        parts = []
        for place, part in enumerate((high, mid, low)):
            turn = (place * SIDE - start) % HD
            parts.append(pltpu.roll(part, turn, 1) if turn else part)
        merged = jnp.where(lane < 2 * SIDE, parts[1], jnp.where(lane < 3 * SIDE, parts[2], 0.0))
        merged = jnp.where(lane < SIDE, parts[0], merged)
        out_ref[3 * count :, :] = merged.astype(BF16)


def edges(index, tail, lat):
    count = 3 * tail.shape[0]
    shapes = [count] + [count + lat.shape[0]] * 2 + [count] * 6
    vmem = pl.BlockSpec(memory_space=VMEM)
    return pl.pallas_call(
        edges_kernel,
        in_specs=[pl.BlockSpec(memory_space=pltpu.SMEM), vmem, vmem],
        out_specs=[vmem] * 9,
        out_shape=[jax.ShapeDtypeStruct((lines, HD), BF16) for lines in shapes],
        compiler_params=pltpu.CompilerParams(vmem_limit_bytes=16 << 20),
        name="edges",
    )(index, tail, lat)


def to_around(arrays):
    rows, bands = lax.axis_size("seq"), lax.axis_size("grp")
    arrived = []
    for (dr, dz), array in zip(AROUND, arrays):
        pairs = [
            (r * bands + z, (r + dr) * bands + z + dz)
            for r in range(max(-dr, 0), rows - max(dr, 0))
            for z in range(max(-dz, 0), bands - max(dz, 0))
        ]
        arrived.append(lax.ppermute(array, ("seq", "grp"), pairs))
    return arrived


STARTS = (((0, 1), (1, 0), (1, 1)), ((0, 0), (0, 1), (1, 0)))


def taps_kernel(w_ref, o_ref):
    out = w_ref.shape[1]
    o_ref[...] = jnp.zeros_like(o_ref)
    for kind, start in enumerate(STARTS):
        for tf in range(3):
            for ti in range(3):
                for tj, (token, b) in enumerate(start):
                    tap = ((tf * 3 + ti) * 3 + tj) * LAT_CH
                    piece = w_ref[tap : tap + LAT_CH, :]
                    for i in range(2):
                        at = tf * 2 * HD + token * HD + (i + ti) * SIDE + b * LAT_CH
                        o_ref[kind, at : at + LAT_CH, i * out : (i + 1) * out] = piece


def spread_taps(conv_weight):
    out = conv_weight.shape[1]
    return pl.pallas_call(
        taps_kernel,
        in_specs=[pl.BlockSpec(memory_space=VMEM)],
        out_specs=pl.BlockSpec(memory_space=VMEM),
        out_shape=jax.ShapeDtypeStruct((2, 6 * HD, 2 * out), BF16),
        compiler_params=pltpu.CompilerParams(vmem_limit_bytes=16 << 20),
        name="spread_taps",
    )(conv_weight)


def conv_kernel(index_ref, z_ref, taps_ref, bias_ref, *refs):
    *cached_refs, o_ref = refs
    videos, lines, _ = z_ref.shape
    frames = lines // 4
    out = bias_ref.shape[1]
    odd = index_ref[0] % 2
    count = videos * frames
    at = lax.broadcasted_iota(jnp.int32, (3 * count, videos * lines), 0)
    source = lax.broadcasted_iota(jnp.int32, (3 * count, videos * lines), 1)
    t, frame, video = at // count, (at // videos) % frames, at % videos
    chosen = jnp.where(source == video * lines + frame * 4 + t, 1.0, 0.0).astype(BF16)
    image = dot_nn(chosen, z_ref[...].reshape(videos * lines, HD)).astype(BF16)
    held = cached_refs[0].shape[0] // 3
    cached = sum(ref[: 3 * held, :].astype(F32) for ref in cached_refs).astype(BF16)
    token = [
        jnp.concatenate(
            [cached[t * held : (t + 1) * held], image[t * count : (t + 1) * count]], axis=0
        )
        for t in range(3)
    ]

    def windows(first, second):
        wide = jnp.concatenate([first, second], axis=1)
        return jnp.concatenate([wide[tf * videos : tf * videos + count] for tf in range(3)], axis=1)

    middle = jnp.where(odd == 1, windows(token[0], token[1]), windows(token[1], token[2]))
    outer = jnp.concatenate([windows(token[0], token[1]), windows(token[1], token[2])], axis=0)
    outer = dot_nn(outer, taps_ref[odd])
    inner = dot_nn(middle, taps_ref[1 - odd])
    for j, part in enumerate((outer[:count], inner, outer[count:])):
        done = []
        for i in range(2):
            conv = part[:, i * out : (i + 1) * out] + bias_ref[...]
            mean_sq = jnp.mean(conv * conv, axis=1, keepdims=True)
            normed = conv / jnp.sqrt(mean_sq + NORM_EPS)
            done.append(normed / (1.0 + jnp.exp(-normed)))
        for f in range(frames):
            at = slice(f * videos, (f + 1) * videos)
            tile = jnp.concatenate([d[at][:, None, :] for d in done], axis=1)
            o_ref[:, f, j] = tile.astype(BF16)


def convolve(index, z, cached, taps, bias):
    videos, lines, _ = z.shape
    out = bias.shape[1]
    vmem = pl.BlockSpec(memory_space=VMEM)
    return pl.pallas_call(
        conv_kernel,
        in_specs=[pl.BlockSpec(memory_space=pltpu.SMEM)] + [vmem] * (3 + len(cached)),
        out_specs=vmem,
        out_shape=jax.ShapeDtypeStruct((videos, lines // 4, 3, 2, out), BF16),
        compiler_params=pltpu.CompilerParams(vmem_limit_bytes=32 << 20),
        name="convolve",
    )(index, z, taps, bias, *cached).transpose(0, 1, 3, 2, 4)


def on_device(
    query,
    key_states,
    value_states,
    latent,
    sigma,
    head_weight,
    latent_scale,
    latent_shift,
    frame_tail,
    conv_weight,
    conv_bias,
):
    features = query.shape[4]
    heads = features // HD
    frames, cols = latent.shape[2], latent.shape[3]
    rows = frames * cols
    bands = lax.axis_size("grp")
    seq_at, grp_at = lax.axis_index("seq"), lax.axis_index("grp")
    videos, tail_frames = frame_tail.shape[0], frame_tail.shape[1]

    sent = pack_heads(
        query.reshape(rows, features),
        key_states.reshape(rows, features),
        value_states.reshape(rows, features),
        heads,
    )
    mine = lax.all_to_all(sent, "seq", 0, 0, tiled=True)

    seq_at, grp_at = seq_at.reshape(1), grp_at.reshape(1)
    lat = jnp.pad(latent.reshape(rows, 4 * LAT_CH), ((0, 0), (SIDE, SIDE)))
    tail = jnp.transpose(frame_tail, (1, 0, 2, 3, 4)).reshape(videos * tail_frames, -1)
    own, *sides = edges(grp_at, tail, lat)
    sides = to_around(sides)

    taps = spread_taps(conv_weight)
    w = lax.dynamic_slice_in_dim(head_weight, seq_at[0] * HD, HD, axis=0)
    w = jnp.concatenate([w[:, SIDE:], w, w[:, :SIDE]], axis=1)
    gain = jnp.tile(latent_scale, HD // LAT_CH).reshape(1, HD)
    shift = jnp.tile(latent_shift, HD // LAT_CH).reshape(1, HD)

    bias = conv_bias.reshape(1, -1)
    mine, w, lat, own, sides, taps, gain, shift, bias, sigma = lax.optimization_barrier(
        (mine, w, lat, own, sides, taps, gain, shift, bias, sigma)
    )

    parts = lax.all_to_all(attend(mine, w), "seq", 0, 0, tiled=True)
    bands_out = update(
        seq_at, sigma, parts, lat, sides[0], sides[1], gain, shift, features, bands
    )
    tiles = lax.all_to_all(bands_out, "grp", 0, 0, tiled=True)
    return convolve(grp_at, tiles, [own] + sides, taps, bias)


def solution(mesh):
    return jax.shard_map(
        on_device,
        mesh=mesh,
        in_specs=(
            P("grp", "seq", None, None, None),
            P("grp", "seq", None, None, None),
            P("grp", "seq", None, None, None),
            P("grp", "seq", None, None, None),
            P("grp"),
            P(),
            P(),
            P(),
            P(None, None, "seq", "grp", None),
            P(),
            P(),
        ),
        out_specs=P(None, None, "seq", "grp", None),
        check_vma=False,
    )
```

```python
import functools
import math

import jax
import jax.numpy as jnp
import numpy as np
from jax import lax
from jax.experimental import pallas as pl
from jax.experimental.pallas import tpu as pltpu
from jax.sharding import PartitionSpec as P

HD = 128
LAT_CH = 16
NORM_EPS = 1e-06
F32 = jnp.float32
BF16 = jnp.bfloat16
VMEM = pltpu.VMEM
SIDE = 2 * LAT_CH


def dot_nt(a, b):
    return lax.dot_general(a, b, (((1,), (1,)), ((), ())), preferred_element_type=F32)


def dot_nn(a, b):
    return jnp.dot(a, b, preferred_element_type=F32)


def pack_kernel(q_ref, k_ref, v_ref, o_ref):
    rows = q_ref.shape[0]
    for place, ref in enumerate((q_ref, k_ref, v_ref)):
        for head in range(o_ref.shape[0]):
            o_ref[head, place * rows : (place + 1) * rows, :] = ref[:, head * HD : (head + 1) * HD]


def pack_heads(query, keys, values, heads, steps=2):
    rows, features = query.shape
    width = features // steps
    spec = pl.BlockSpec((rows, width), lambda i: (0, i))
    return pl.pallas_call(
        pack_kernel,
        grid=(steps,),
        in_specs=[spec] * 3,
        out_specs=pl.BlockSpec((heads // steps, 3 * rows, HD), lambda i: (i, 0, 0)),
        out_shape=jax.ShapeDtypeStruct((heads, 3 * rows, HD), BF16),
        name="pack_heads",
    )(query, keys, values)


def attend_kernel(
    block_tr, x_ref, w_ref, o_ref, queries, keys, kk, vx, held, vel, ssq, msg, sems, *buffers
):
    tr, rows3, _ = x_ref.shape
    rows = rows3 // 3
    into = (queries, keys, vx.at[:, :, :HD])
    fetches = [
        pltpu.make_async_copy(x_ref.at[:, n * rows : (n + 1) * rows, :], into[n], sems.at[n])
        for n in range(3)
    ]
    for n in (1, 0, 2):
        fetches[n].start()
    tokens, block = tr * rows, block_tr * rows
    steps = tr // block_tr
    factor = math.log2(math.e) / math.sqrt(HD)
    chunk_tr = 8
    chunk = chunk_tr * rows

    def score(step):
        s_ref, peak_ref = buffers[step % 2], buffers[2 + step % 2]
        q = queries[step * block_tr : (step + 1) * block_tr].reshape(block, HD)
        q = q.astype(F32) * factor
        high = q.astype(BF16)
        q = jnp.concatenate([high, (q - high.astype(F32)).astype(BF16)], axis=1)
        peak = None
        for c in range(tr // chunk_tr):
            at = slice(c * chunk, (c + 1) * chunk)
            if step == 0:
                piece = keys[c * chunk_tr : (c + 1) * chunk_tr]
                flipped = piece.reshape(chunk, HD).astype(F32).T.astype(BF16)
                kk[:HD, at] = flipped
                kk[HD:, at] = flipped
            s = dot_nn(q, kk[:, at])
            s_ref[:, at] = s
            for l in range(0, chunk, HD):
                part = s[:, l : l + HD]
                peak = part if peak is None else jnp.maximum(peak, part)
        peak_ref[...] = jnp.broadcast_to(jnp.max(peak, axis=1, keepdims=True), peak_ref.shape)

    def mix(step):
        s_ref, peak_ref = buffers[step % 2], buffers[2 + step % 2]
        peak = peak_ref[...]
        weights = jnp.concatenate(
            [
                jnp.exp2(s_ref[:, l : l + HD] - peak).astype(BF16)
                for l in range(0, tokens, HD)
            ],
            axis=1,
        )
        mixed = dot_nn(weights, vx[...].reshape(tokens, 2 * HD))
        held[step * block : (step + 1) * block, :] = (mixed[:, :HD] / mixed[:, HD:]).astype(BF16)

    lane = lax.broadcasted_iota(jnp.int32, (rows, HD), 1)
    line = lax.broadcasted_iota(jnp.int32, (16, HD), 0)

    def send(r):
        up, down = (r - 1) % tr, (r + 1) % tr
        piece = [vel[t * rows : (t + 1) * rows, :] for t in (up, r, down)]
        merged = jnp.where(lane < SIDE, piece[0], jnp.where(lane < 3 * SIDE, piece[1], piece[2]))
        msg[r, :rows, :] = merged.astype(BF16)
        merged = jnp.where(line == 0, ssq[up], jnp.where(line == 1, ssq[r], ssq[down]))
        msg[r, rows:, :] = merged.astype(BF16)
        pltpu.make_async_copy(msg.at[r], o_ref.at[r], sems.at[3]).start()

    ssq[...] = jnp.zeros_like(ssq)
    fetches[1].wait()
    fetches[0].wait()
    score(0)
    fetches[2].wait()
    vx[:, :, HD:] = jnp.ones((tr, rows, HD), BF16)
    for step in range(steps):
        if step + 1 < steps:
            score(step + 1)
        mix(step)
    vel[...] = dot_nn(held[...], w_ref[...])
    for r in range(tr):
        wide = held[r * rows : (r + 1) * rows, :].astype(F32)
        ssq[r, :, :rows] = dot_nt(jnp.ones((16, HD), BF16), (wide * wide).astype(BF16))
    for r in range(tr):
        send(r)
    pltpu.make_async_copy(msg, o_ref, sems.at[3]).wait()


def attend(x, w, block_tr=4):
    tr, rows3, _ = x.shape
    rows = rows3 // 3
    tokens, block = tr * rows, block_tr * rows
    return pl.pallas_call(
        functools.partial(attend_kernel, block_tr),
        in_specs=[pl.BlockSpec(memory_space=pl.ANY), pl.BlockSpec(memory_space=VMEM)],
        out_specs=pl.BlockSpec(memory_space=pltpu.HBM),
        out_shape=pltpu.HBM((tr, rows + 16, HD), BF16),
        scratch_shapes=[
            VMEM((tr, rows, HD), BF16),
            VMEM((tr, rows, HD), BF16),
            VMEM((2 * HD, tokens), BF16),
            VMEM((tr, rows, 2 * HD), BF16),
            VMEM((tokens, HD), BF16),
            VMEM((tokens, HD), F32),
            VMEM((tr, 16, HD), F32),
            VMEM((tr, rows + 16, HD), BF16),
            pltpu.SemaphoreType.DMA((4,)),
            VMEM((block, tokens), F32),
            VMEM((block, tokens), F32),
            VMEM((block, HD), F32),
            VMEM((block, HD), F32),
        ],
        compiler_params=pltpu.CompilerParams(vmem_limit_bytes=32 << 20),
        cost_estimate=pl.CostEstimate(
            flops=8 * tokens * tokens * HD, bytes_accessed=4 << 20, transcendentals=tokens * tokens
        ),
        name="attend",
    )(x, w)


def update_kernel(
    features, bands, index_ref, sigma_ref, y_ref, lat_ref, above_ref, below_ref, gain_ref, shift_ref, o_ref
):
    heads, lines, _ = y_ref.shape
    rows = lines - 16
    frames = 4
    cols = rows // frames
    total = y_ref[0].astype(F32)
    for h in range(1, heads):
        total = total + y_ref[h].astype(F32)
    velocity = total[:rows]
    sums = jnp.concatenate([total[rows:], jnp.zeros((HD - 16, HD), F32)], axis=0).T
    lane = lax.broadcasted_iota(jnp.int32, (rows, HD), 1)
    up, own, down = (jnp.broadcast_to(sums[:rows, i : i + 1], (rows, HD)) for i in range(3))
    square = jnp.where(lane < SIDE, up, jnp.where(lane < 3 * SIDE, own, down))
    velocity = velocity / jnp.sqrt(square * (1.0 / features) + NORM_EPS)
    above = above_ref[above_ref.shape[0] - rows :, :].astype(F32)
    below = below_ref[below_ref.shape[0] - rows :, :].astype(F32)
    above = above + pltpu.roll(above, HD - SIDE, 1) + pltpu.roll(above, HD - 2 * SIDE, 1)
    below = pltpu.roll(below, 3 * SIDE, 1) + pltpu.roll(below, 2 * SIDE, 1) + pltpu.roll(below, SIDE, 1)
    lat = jnp.where(lane < SIDE, above, jnp.where(lane < 3 * SIDE, lat_ref[...], below))
    cleaned = lat - sigma_ref[0] * velocity
    scaled = cleaned * gain_ref[...] + shift_ref[...]
    first, last = index_ref[0] == 0, index_ref[0] == heads - 1
    drop = ((lane < SIDE) & first) | ((lane >= 3 * SIDE) & last)
    scaled = jnp.where(drop, 0.0, scaled).astype(BF16)
    count = bands * 4 * frames
    at = lax.broadcasted_iota(jnp.int32, (count, rows), 0)
    source = lax.broadcasted_iota(jnp.int32, (count, rows), 1)
    band, frame, t = at // (4 * frames), (at // 4) % frames, at % 4
    column = (3 * band + 1) // 2 - 1 + t
    hit = (source == frame * cols + column) & (column >= 0) & (column < cols)
    chosen = jnp.where(hit, 1.0, 0.0).astype(BF16)
    o_ref[...] = dot_nn(chosen, scaled).astype(BF16).reshape(o_ref.shape)


def update(index, sigma, y, lat, above, below, gain, shift, features, bands):
    smem = pl.BlockSpec(memory_space=pltpu.SMEM)
    vmem = pl.BlockSpec(memory_space=VMEM)
    return pl.pallas_call(
        functools.partial(update_kernel, features, bands),
        in_specs=[smem, smem] + [vmem] * 6,
        out_specs=vmem,
        out_shape=jax.ShapeDtypeStruct((bands, 16, HD), BF16),
        compiler_params=pltpu.CompilerParams(vmem_limit_bytes=16 << 20),
        name="update",
    )(index, sigma, y, lat, above, below, gain, shift)


def columns_kernel(index_ref, tail_ref, own_ref, right_ref, left_ref):
    count, width = tail_ref.shape
    odd = index_ref[0] % 2
    shape = (width, 3 * HD)
    k = lax.broadcasted_iota(jnp.int32, shape, 0)
    n = lax.broadcasted_iota(jnp.int32, shape, 1)
    pixel = k // LAT_CH
    i = jnp.where(pixel >= 3, 1, 0)
    j = pixel - 3 * i
    same = ((k % LAT_CH) == (n % LAT_CH)) & ((n % HD) // SIDE == i + 1)
    slot = 2 * (n // HD) + (n % SIDE) // LAT_CH
    for dz, out_ref in ((0, own_ref), (1, right_ref), (-1, left_ref)):
        shift = 1 - odd if dz == 0 else odd
        hit = same & (slot == j + (1 - 3 * dz) + shift)
        if dz:
            hit = hit & (j == (2 if dz == 1 else 0))
        placed = dot_nn(tail_ref[...], jnp.where(hit, 1.0, 0.0).astype(BF16)).astype(BF16)
        for t in range(3):
            out_ref[t * count : (t + 1) * count, :] = placed[:, t * HD : (t + 1) * HD]


def rows_kernel(own_ref, before_ref, after_ref, lat_ref, tile_ref, down_ref, up_ref):
    tile = own_ref[...].astype(F32) + before_ref[...].astype(F32) + after_ref[...].astype(F32)
    count = tile.shape[0]
    tile_ref[...] = tile.astype(BF16)
    lane = lax.broadcasted_iota(jnp.int32, tile.shape, 1)
    turned = pltpu.roll(tile, 2 * SIDE, 1)
    down_ref[:count, :] = jnp.where(lane < SIDE, turned, 0.0).astype(BF16)
    up_ref[:count, :] = jnp.where(lane >= 3 * SIDE, turned, 0.0).astype(BF16)
    lat = lat_ref[...]
    high = lat.astype(BF16).astype(F32)
    rest = lat - high
    mid = rest.astype(BF16).astype(F32)
    low = rest - mid
    lane = lax.broadcasted_iota(jnp.int32, lat.shape, 1)
    for out_ref, start in ((down_ref, 2 * SIDE), (up_ref, SIDE)):
        parts = []
        for place, part in enumerate((high, mid, low)):
            turn = (place * SIDE - start) % HD
            parts.append(pltpu.roll(part, turn, 1) if turn else part)
        merged = jnp.where(lane < 2 * SIDE, parts[1], jnp.where(lane < 3 * SIDE, parts[2], 0.0))
        merged = jnp.where(lane < SIDE, parts[0], merged)
        out_ref[count:, :] = merged.astype(BF16)


def edges(index, tail, lat):
    count, more = 3 * tail.shape[0], lat.shape[0]
    vmem = pl.BlockSpec(memory_space=VMEM)
    tile = jax.ShapeDtypeStruct((count, HD), BF16)
    both = jax.ShapeDtypeStruct((count + more, HD), BF16)
    small = pltpu.CompilerParams(vmem_limit_bytes=8 << 20)
    own, right, left = pl.pallas_call(
        columns_kernel,
        in_specs=[pl.BlockSpec(memory_space=pltpu.SMEM), vmem],
        out_specs=[vmem] * 3,
        out_shape=[tile] * 3,
        compiler_params=small,
        name="edge_columns",
    )(index, tail)
    before, after = to_next(right, "grp"), to_last(left, "grp")
    own, down, up = pl.pallas_call(
        rows_kernel,
        in_specs=[vmem] * 4,
        out_specs=[vmem] * 3,
        out_shape=[tile, both, both],
        compiler_params=small,
        name="edge_rows",
    )(own, before, after, lat)
    return own, to_next(down, "seq"), to_last(up, "seq")


def to_next(array, axis):
    return lax.ppermute(array, axis, [(i, i + 1) for i in range(lax.axis_size(axis) - 1)])


def to_last(array, axis):
    return lax.ppermute(array, axis, [(i + 1, i) for i in range(lax.axis_size(axis) - 1)])


STARTS = (((0, 1), (1, 0), (1, 1)), ((0, 0), (0, 1), (1, 0)))


def taps_kernel(w_ref, o_ref):
    out = w_ref.shape[1]
    o_ref[...] = jnp.zeros_like(o_ref)
    for kind, start in enumerate(STARTS):
        for tf in range(3):
            for ti in range(3):
                for tj, (token, b) in enumerate(start):
                    tap = ((tf * 3 + ti) * 3 + tj) * LAT_CH
                    piece = w_ref[tap : tap + LAT_CH, :]
                    for i in range(2):
                        at = tf * 2 * HD + token * HD + (i + ti) * SIDE + b * LAT_CH
                        o_ref[kind, at : at + LAT_CH, i * out : (i + 1) * out] = piece


def spread_taps(conv_weight):
    out = conv_weight.shape[1]
    return pl.pallas_call(
        taps_kernel,
        in_specs=[pl.BlockSpec(memory_space=VMEM)],
        out_specs=pl.BlockSpec(memory_space=VMEM),
        out_shape=jax.ShapeDtypeStruct((2, 6 * HD, 2 * out), BF16),
        compiler_params=pltpu.CompilerParams(vmem_limit_bytes=8 << 20),
        name="spread_taps",
    )(conv_weight)


def conv_kernel(index_ref, z_ref, own_ref, above_ref, below_ref, taps_ref, bias_ref, o_ref):
    videos, lines, _ = z_ref.shape
    frames = lines // 4
    out = bias_ref.shape[1]
    odd = index_ref[0] % 2
    count = videos * frames
    at = lax.broadcasted_iota(jnp.int32, (3 * count, videos * lines), 0)
    source = lax.broadcasted_iota(jnp.int32, (3 * count, videos * lines), 1)
    t, frame, video = at // count, (at // videos) % frames, at % videos
    chosen = jnp.where(source == video * lines + frame * 4 + t, 1.0, 0.0).astype(BF16)
    image = dot_nn(chosen, z_ref[...].reshape(videos * lines, HD)).astype(BF16)
    cached = own_ref[...].astype(F32)
    for ref in (above_ref, below_ref):
        cached = cached + ref[: cached.shape[0], :].astype(F32)
    cached = cached.astype(BF16)
    held = cached.shape[0] // 3
    token = [
        jnp.concatenate(
            [cached[t * held : (t + 1) * held], image[t * count : (t + 1) * count]], axis=0
        )
        for t in range(3)
    ]

    def windows(first, second):
        wide = jnp.concatenate([first, second], axis=1)
        return jnp.concatenate([wide[tf * videos : tf * videos + count] for tf in range(3)], axis=1)

    middle = jnp.where(odd == 1, windows(token[0], token[1]), windows(token[1], token[2]))
    outer = jnp.concatenate([windows(token[0], token[1]), windows(token[1], token[2])], axis=0)
    outer = dot_nn(outer, taps_ref[odd])
    inner = dot_nn(middle, taps_ref[1 - odd])
    for j, part in enumerate((outer[:count], inner, outer[count:])):
        done = []
        for i in range(2):
            conv = part[:, i * out : (i + 1) * out] + bias_ref[...]
            mean_sq = jnp.mean(conv * conv, axis=1, keepdims=True)
            normed = conv / jnp.sqrt(mean_sq + NORM_EPS)
            done.append(normed / (1.0 + jnp.exp(-normed)))
        for f in range(frames):
            at = slice(f * videos, (f + 1) * videos)
            tile = jnp.concatenate([d[at][:, None, :] for d in done], axis=1)
            o_ref[:, f, j] = tile.astype(BF16)


def convolve(index, z, own, above, below, taps, bias):
    videos, lines, _ = z.shape
    out = bias.shape[1]
    vmem = pl.BlockSpec(memory_space=VMEM)
    return pl.pallas_call(
        conv_kernel,
        in_specs=[pl.BlockSpec(memory_space=pltpu.SMEM)] + [vmem] * 6,
        out_specs=vmem,
        out_shape=jax.ShapeDtypeStruct((videos, lines // 4, 3, 2, out), BF16),
        compiler_params=pltpu.CompilerParams(vmem_limit_bytes=16 << 20),
        name="convolve",
    )(index, z, own, above, below, taps, bias).transpose(0, 1, 3, 2, 4)


def on_device(
    query,
    key_states,
    value_states,
    latent,
    sigma,
    head_weight,
    latent_scale,
    latent_shift,
    frame_tail,
    conv_weight,
    conv_bias,
):
    features = query.shape[4]
    heads = features // HD
    frames, cols = latent.shape[2], latent.shape[3]
    rows = frames * cols
    bands = lax.axis_size("grp")
    seq_at, grp_at = lax.axis_index("seq"), lax.axis_index("grp")
    videos, tail_frames = frame_tail.shape[0], frame_tail.shape[1]

    sent = pack_heads(
        query.reshape(rows, features),
        key_states.reshape(rows, features),
        value_states.reshape(rows, features),
        heads,
    )
    mine = lax.all_to_all(sent, "seq", 0, 0, tiled=True)

    seq_at, grp_at = seq_at.reshape(1), grp_at.reshape(1)
    lat = jnp.pad(latent.reshape(rows, 4 * LAT_CH), ((0, 0), (SIDE, SIDE)))
    tail = jnp.transpose(frame_tail, (1, 0, 2, 3, 4)).reshape(videos * tail_frames, -1)
    own, above, below = edges(grp_at, tail, lat)

    taps = spread_taps(conv_weight)
    w = lax.dynamic_slice_in_dim(head_weight, seq_at[0] * HD, HD, axis=0)
    w = jnp.concatenate([w[:, SIDE:], w, w[:, :SIDE]], axis=1)
    gain = jnp.tile(latent_scale, HD // LAT_CH).reshape(1, HD)
    shift = jnp.tile(latent_shift, HD // LAT_CH).reshape(1, HD)

    bias = conv_bias.reshape(1, -1)
    mine, w, lat, own, above, below, taps, gain, shift, bias, sigma = lax.optimization_barrier(
        (mine, w, lat, own, above, below, taps, gain, shift, bias, sigma)
    )

    parts = lax.all_to_all(attend(mine, w), "seq", 0, 0, tiled=True)
    bands_out = update(seq_at, sigma, parts, lat, above, below, gain, shift, features, bands)
    tiles = lax.all_to_all(bands_out, "grp", 0, 0, tiled=True)
    return convolve(grp_at, tiles, own, above, below, taps, bias)


def solution(mesh):
    return jax.shard_map(
        on_device,
        mesh=mesh,
        in_specs=(
            P("grp", "seq", None, None, None),
            P("grp", "seq", None, None, None),
            P("grp", "seq", None, None, None),
            P("grp", "seq", None, None, None),
            P("grp"),
            P(),
            P(),
            P(),
            P(None, None, "seq", "grp", None),
            P(),
            P(),
        ),
        out_specs=P(None, None, "seq", "grp", None),
        check_vma=False,
    )
```

```python
import functools
import math

import jax
import jax.numpy as jnp
import numpy as np
from jax import lax
from jax.experimental import pallas as pl
from jax.experimental.pallas import tpu as pltpu
from jax.sharding import PartitionSpec as P

HD = 128
LAT_CH = 16
NORM_EPS = 1e-06
F32 = jnp.float32
BF16 = jnp.bfloat16
VMEM = pltpu.VMEM
SIDE = 2 * LAT_CH


def dot_nt(a, b):
    return lax.dot_general(a, b, (((1,), (1,)), ((), ())), preferred_element_type=F32)


def dot_nn(a, b):
    return jnp.dot(a, b, preferred_element_type=F32)


def pack_kernel(q_ref, k_ref, v_ref, o_ref):
    rows = q_ref.shape[0]
    for place, ref in enumerate((q_ref, k_ref, v_ref)):
        for head in range(o_ref.shape[0]):
            o_ref[head, place * rows : (place + 1) * rows, :] = ref[:, head * HD : (head + 1) * HD]


def pack_heads(query, keys, values, heads, steps=2):
    rows, features = query.shape
    width = features // steps
    spec = pl.BlockSpec((rows, width), lambda i: (0, i))
    return pl.pallas_call(
        pack_kernel,
        grid=(steps,),
        in_specs=[spec] * 3,
        out_specs=pl.BlockSpec((heads // steps, 3 * rows, HD), lambda i: (i, 0, 0)),
        out_shape=jax.ShapeDtypeStruct((heads, 3 * rows, HD), BF16),
        name="pack_heads",
    )(query, keys, values)


def attend_kernel(
    block_tr, x_ref, w_ref, o_ref, queries, keys, kk, vx, held, vel, ssq, sems, *buffers
):
    tr, rows3, _ = x_ref.shape
    rows = rows3 // 3
    into = (queries, keys, vx.at[:, :, :HD])
    fetches = [
        pltpu.make_async_copy(x_ref.at[:, n * rows : (n + 1) * rows, :], into[n], sems.at[n])
        for n in range(3)
    ]
    for n in (1, 0, 2):
        fetches[n].start()
    tokens, block = tr * rows, block_tr * rows
    steps = tr // block_tr
    factor = math.log2(math.e) / math.sqrt(HD)
    chunk_tr = 8
    chunk = chunk_tr * rows

    def score(step):
        s_ref, peak_ref = buffers[step % 2], buffers[2 + step % 2]
        q = queries[step * block_tr : (step + 1) * block_tr].reshape(block, HD)
        q = q.astype(F32) * factor
        high = q.astype(BF16)
        q = jnp.concatenate([high, (q - high.astype(F32)).astype(BF16)], axis=1)
        peak = None
        for c in range(tr // chunk_tr):
            at = slice(c * chunk, (c + 1) * chunk)
            if step == 0:
                piece = keys[c * chunk_tr : (c + 1) * chunk_tr]
                flipped = piece.reshape(chunk, HD).astype(F32).T.astype(BF16)
                kk[:HD, at] = flipped
                kk[HD:, at] = flipped
            s = dot_nn(q, kk[:, at])
            s_ref[:, at] = s
            for l in range(0, chunk, HD):
                part = s[:, l : l + HD]
                peak = part if peak is None else jnp.maximum(peak, part)
        peak_ref[...] = jnp.broadcast_to(jnp.max(peak, axis=1, keepdims=True), peak_ref.shape)

    def mix(step):
        s_ref, peak_ref = buffers[step % 2], buffers[2 + step % 2]
        peak = peak_ref[...]
        weights = jnp.concatenate(
            [
                jnp.exp2(s_ref[:, l : l + HD] - peak).astype(BF16)
                for l in range(0, tokens, HD)
            ],
            axis=1,
        )
        mixed = dot_nn(weights, vx[...].reshape(tokens, 2 * HD))
        held[step * block : (step + 1) * block, :] = (mixed[:, :HD] / mixed[:, HD:]).astype(BF16)

    lane = lax.broadcasted_iota(jnp.int32, (rows, HD), 1)
    line = lax.broadcasted_iota(jnp.int32, (16, HD), 0)

    def send(r):
        up, down = (r - 1) % tr, (r + 1) % tr
        piece = [vel[t * rows : (t + 1) * rows, :] for t in (up, r, down)]
        merged = jnp.where(lane < SIDE, piece[0], jnp.where(lane < 3 * SIDE, piece[1], piece[2]))
        o_ref[r, :rows, :] = merged.astype(BF16)
        merged = jnp.where(line == 0, ssq[up], jnp.where(line == 1, ssq[r], ssq[down]))
        o_ref[r, rows:, :] = merged.astype(BF16)

    ssq[...] = jnp.zeros_like(ssq)
    fetches[1].wait()
    fetches[0].wait()
    score(0)
    fetches[2].wait()
    vx[:, :, HD:] = jnp.ones((tr, rows, HD), BF16)
    for step in range(steps):
        if step + 1 < steps:
            score(step + 1)
        mix(step)
    vel[...] = dot_nn(held[...], w_ref[...])
    wide = held[...].astype(F32)
    total = dot_nt(jnp.ones((16, HD), BF16), (wide * wide).astype(BF16))
    for r in range(tr):
        ssq[r, :, :rows] = total[:, r * rows : (r + 1) * rows]
    for r in range(tr):
        send(r)


def attend(x, w, block_tr=4):
    tr, rows3, _ = x.shape
    rows = rows3 // 3
    tokens, block = tr * rows, block_tr * rows
    return pl.pallas_call(
        functools.partial(attend_kernel, block_tr),
        in_specs=[pl.BlockSpec(memory_space=pl.ANY), pl.BlockSpec(memory_space=VMEM)],
        out_specs=pl.BlockSpec(memory_space=VMEM),
        out_shape=jax.ShapeDtypeStruct((tr, rows + 16, HD), BF16),
        scratch_shapes=[
            VMEM((tr, rows, HD), BF16),
            VMEM((tr, rows, HD), BF16),
            VMEM((2 * HD, tokens), BF16),
            VMEM((tr, rows, 2 * HD), BF16),
            VMEM((tokens, HD), BF16),
            VMEM((tokens, HD), F32),
            VMEM((tr, 16, HD), F32),
            pltpu.SemaphoreType.DMA((3,)),
            VMEM((block, tokens), F32),
            VMEM((block, tokens), F32),
            VMEM((block, HD), F32),
            VMEM((block, HD), F32),
        ],
        compiler_params=pltpu.CompilerParams(vmem_limit_bytes=32 << 20),
        cost_estimate=pl.CostEstimate(
            flops=8 * tokens * tokens * HD, bytes_accessed=4 << 20, transcendentals=tokens * tokens
        ),
        name="attend",
    )(x, w)


def update_kernel(
    features, bands, index_ref, y_ref, lat_ref, above_ref, below_ref, sigma_ref, gain_ref, shift_ref, o_ref
):
    heads, lines, _ = y_ref.shape
    rows = lines - 16
    frames = 4
    cols = rows // frames
    total = y_ref[0].astype(F32)
    for h in range(1, heads):
        total = total + y_ref[h].astype(F32)
    velocity = total[:rows]
    sums = jnp.concatenate([total[rows:], jnp.zeros((HD - 16, HD), F32)], axis=0).T
    lane = lax.broadcasted_iota(jnp.int32, (rows, HD), 1)
    up, own, down = (jnp.broadcast_to(sums[:rows, i : i + 1], (rows, HD)) for i in range(3))
    square = jnp.where(lane < SIDE, up, jnp.where(lane < 3 * SIDE, own, down))
    velocity = velocity / jnp.sqrt(square * (1.0 / features) + NORM_EPS)
    above = above_ref[above_ref.shape[0] - rows :, :].astype(F32)
    below = below_ref[below_ref.shape[0] - rows :, :].astype(F32)
    above = above + pltpu.roll(above, HD - SIDE, 1) + pltpu.roll(above, HD - 2 * SIDE, 1)
    below = pltpu.roll(below, 3 * SIDE, 1) + pltpu.roll(below, 2 * SIDE, 1) + pltpu.roll(below, SIDE, 1)
    lat = jnp.where(lane < SIDE, above, jnp.where(lane < 3 * SIDE, lat_ref[...], below))
    cleaned = lat - sigma_ref[...] * velocity
    scaled = cleaned * gain_ref[...] + shift_ref[...]
    first, last = index_ref[0] == 0, index_ref[0] == heads - 1
    drop = ((lane < SIDE) & first) | ((lane >= 3 * SIDE) & last)
    scaled = jnp.where(drop, 0.0, scaled).astype(BF16)
    count = bands * 4 * frames
    at = lax.broadcasted_iota(jnp.int32, (count, rows), 0)
    source = lax.broadcasted_iota(jnp.int32, (count, rows), 1)
    band, frame, t = at // (4 * frames), (at // 4) % frames, at % 4
    column = (3 * band + 1) // 2 - 1 + t
    hit = (source == frame * cols + column) & (column >= 0) & (column < cols)
    chosen = jnp.where(hit, 1.0, 0.0).astype(BF16)
    o_ref[...] = dot_nn(chosen, scaled).astype(BF16).reshape(o_ref.shape)


def update(index, y, lat, above, below, sigma, gain, shift, features, bands):
    smem = pl.BlockSpec(memory_space=pltpu.SMEM)
    vmem = pl.BlockSpec(memory_space=VMEM)
    return pl.pallas_call(
        functools.partial(update_kernel, features, bands),
        in_specs=[smem] + [vmem] * 7,
        out_specs=vmem,
        out_shape=jax.ShapeDtypeStruct((bands, 16, HD), BF16),
        compiler_params=pltpu.CompilerParams(vmem_limit_bytes=16 << 20),
        name="update",
    )(index, y, lat, above, below, sigma, gain, shift)


def columns_kernel(index_ref, tail_ref, own_ref, right_ref, left_ref):
    count, width = tail_ref.shape
    odd = index_ref[0] % 2
    shape = (width, 3 * HD)
    k = lax.broadcasted_iota(jnp.int32, shape, 0)
    n = lax.broadcasted_iota(jnp.int32, shape, 1)
    pixel = k // LAT_CH
    i = jnp.where(pixel >= 3, 1, 0)
    j = pixel - 3 * i
    same = ((k % LAT_CH) == (n % LAT_CH)) & ((n % HD) // SIDE == i + 1)
    slot = 2 * (n // HD) + (n % SIDE) // LAT_CH
    for dz, out_ref in ((0, own_ref), (1, right_ref), (-1, left_ref)):
        shift = 1 - odd if dz == 0 else odd
        hit = same & (slot == j + (1 - 3 * dz) + shift)
        if dz:
            hit = hit & (j == (2 if dz == 1 else 0))
        placed = dot_nn(tail_ref[...], jnp.where(hit, 1.0, 0.0).astype(BF16)).astype(BF16)
        for t in range(3):
            out_ref[t * count : (t + 1) * count, :] = placed[:, t * HD : (t + 1) * HD]


def rows_kernel(own_ref, before_ref, after_ref, lat_ref, tile_ref, down_ref, up_ref):
    tile = own_ref[...].astype(F32) + before_ref[...].astype(F32) + after_ref[...].astype(F32)
    count = tile.shape[0]
    tile_ref[...] = tile.astype(BF16)
    lane = lax.broadcasted_iota(jnp.int32, tile.shape, 1)
    turned = pltpu.roll(tile, 2 * SIDE, 1)
    down_ref[:count, :] = jnp.where(lane < SIDE, turned, 0.0).astype(BF16)
    up_ref[:count, :] = jnp.where(lane >= 3 * SIDE, turned, 0.0).astype(BF16)
    lat = lat_ref[...]
    high = lat.astype(BF16).astype(F32)
    rest = lat - high
    mid = rest.astype(BF16).astype(F32)
    low = rest - mid
    lane = lax.broadcasted_iota(jnp.int32, lat.shape, 1)
    for out_ref, start in ((down_ref, 2 * SIDE), (up_ref, SIDE)):
        parts = []
        for place, part in enumerate((high, mid, low)):
            turn = (place * SIDE - start) % HD
            parts.append(pltpu.roll(part, turn, 1) if turn else part)
        merged = jnp.where(lane < 2 * SIDE, parts[1], jnp.where(lane < 3 * SIDE, parts[2], 0.0))
        merged = jnp.where(lane < SIDE, parts[0], merged)
        out_ref[count:, :] = merged.astype(BF16)


def edges(index, tail, lat):
    count, more = 3 * tail.shape[0], lat.shape[0]
    vmem = pl.BlockSpec(memory_space=VMEM)
    tile = jax.ShapeDtypeStruct((count, HD), BF16)
    both = jax.ShapeDtypeStruct((count + more, HD), BF16)
    small = pltpu.CompilerParams(vmem_limit_bytes=8 << 20)
    own, right, left = pl.pallas_call(
        columns_kernel,
        in_specs=[pl.BlockSpec(memory_space=pltpu.SMEM), vmem],
        out_specs=[vmem] * 3,
        out_shape=[tile] * 3,
        compiler_params=small,
        name="edge_columns",
    )(index, tail)
    before, after = to_next(right, "grp"), to_last(left, "grp")
    own, down, up = pl.pallas_call(
        rows_kernel,
        in_specs=[vmem] * 4,
        out_specs=[vmem] * 3,
        out_shape=[tile, both, both],
        compiler_params=small,
        name="edge_rows",
    )(own, before, after, lat)
    return own, to_next(down, "seq"), to_last(up, "seq")


def to_next(array, axis):
    return lax.ppermute(array, axis, [(i, i + 1) for i in range(lax.axis_size(axis) - 1)])


def to_last(array, axis):
    return lax.ppermute(array, axis, [(i + 1, i) for i in range(lax.axis_size(axis) - 1)])


STARTS = (((0, 1), (1, 0), (1, 1)), ((0, 0), (0, 1), (1, 0)))


def taps_kernel(w_ref, o_ref):
    out = w_ref.shape[1]
    o_ref[...] = jnp.zeros_like(o_ref)
    for kind, start in enumerate(STARTS):
        for tf in range(3):
            for ti in range(3):
                for tj, (token, b) in enumerate(start):
                    tap = ((tf * 3 + ti) * 3 + tj) * LAT_CH
                    piece = w_ref[tap : tap + LAT_CH, :]
                    for i in range(2):
                        at = tf * 2 * HD + token * HD + (i + ti) * SIDE + b * LAT_CH
                        o_ref[kind, at : at + LAT_CH, i * out : (i + 1) * out] = piece


def spread_taps(conv_weight):
    out = conv_weight.shape[1]
    return pl.pallas_call(
        taps_kernel,
        in_specs=[pl.BlockSpec(memory_space=VMEM)],
        out_specs=pl.BlockSpec(memory_space=VMEM),
        out_shape=jax.ShapeDtypeStruct((2, 6 * HD, 2 * out), BF16),
        compiler_params=pltpu.CompilerParams(vmem_limit_bytes=8 << 20),
        name="spread_taps",
    )(conv_weight)


def conv_kernel(index_ref, z_ref, own_ref, above_ref, below_ref, taps_ref, bias_ref, o_ref):
    videos, lines, _ = z_ref.shape
    frames = lines // 4
    out = bias_ref.shape[1]
    odd = index_ref[0] % 2
    count = videos * frames
    at = lax.broadcasted_iota(jnp.int32, (3 * count, videos * lines), 0)
    source = lax.broadcasted_iota(jnp.int32, (3 * count, videos * lines), 1)
    t, frame, video = at // count, (at // videos) % frames, at % videos
    chosen = jnp.where(source == video * lines + frame * 4 + t, 1.0, 0.0).astype(BF16)
    image = dot_nn(chosen, z_ref[...].reshape(videos * lines, HD)).astype(BF16)
    cached = own_ref[...].astype(F32)
    for ref in (above_ref, below_ref):
        cached = cached + ref[: cached.shape[0], :].astype(F32)
    cached = cached.astype(BF16)
    held = cached.shape[0] // 3
    token = [
        jnp.concatenate(
            [cached[t * held : (t + 1) * held], image[t * count : (t + 1) * count]], axis=0
        )
        for t in range(3)
    ]

    def windows(first, second):
        wide = jnp.concatenate([first, second], axis=1)
        return jnp.concatenate([wide[tf * videos : tf * videos + count] for tf in range(3)], axis=1)

    middle = jnp.where(odd == 1, windows(token[0], token[1]), windows(token[1], token[2]))
    outer = jnp.concatenate([windows(token[0], token[1]), windows(token[1], token[2])], axis=0)
    outer = dot_nn(outer, taps_ref[odd])
    inner = dot_nn(middle, taps_ref[1 - odd])
    for j, part in enumerate((outer[:count], inner, outer[count:])):
        done = []
        for i in range(2):
            conv = part[:, i * out : (i + 1) * out] + bias_ref[...]
            mean_sq = jnp.mean(conv * conv, axis=1, keepdims=True)
            normed = conv / jnp.sqrt(mean_sq + NORM_EPS)
            done.append(normed / (1.0 + jnp.exp(-normed)))
        for f in range(frames):
            at = slice(f * videos, (f + 1) * videos)
            tile = jnp.concatenate([d[at][:, None, :] for d in done], axis=1)
            o_ref[:, f, j] = tile.astype(BF16)


def convolve(index, z, own, above, below, taps, bias):
    videos, lines, _ = z.shape
    out = bias.shape[1]
    vmem = pl.BlockSpec(memory_space=VMEM)
    return pl.pallas_call(
        conv_kernel,
        in_specs=[pl.BlockSpec(memory_space=pltpu.SMEM)] + [vmem] * 6,
        out_specs=vmem,
        out_shape=jax.ShapeDtypeStruct((videos, lines // 4, 3, 2, out), BF16),
        compiler_params=pltpu.CompilerParams(vmem_limit_bytes=16 << 20),
        name="convolve",
    )(index, z, own, above, below, taps, bias).transpose(0, 1, 3, 2, 4)


def on_device(
    query,
    key_states,
    value_states,
    latent,
    sigma,
    head_weight,
    latent_scale,
    latent_shift,
    frame_tail,
    conv_weight,
    conv_bias,
):
    features = query.shape[4]
    heads = features // HD
    frames, cols = latent.shape[2], latent.shape[3]
    rows = frames * cols
    bands = lax.axis_size("grp")
    seq_at, grp_at = lax.axis_index("seq"), lax.axis_index("grp")
    videos, tail_frames = frame_tail.shape[0], frame_tail.shape[1]

    sent = pack_heads(
        query.reshape(rows, features),
        key_states.reshape(rows, features),
        value_states.reshape(rows, features),
        heads,
    )
    mine = lax.all_to_all(sent, "seq", 0, 0, tiled=True)

    seq_at, grp_at = seq_at.reshape(1), grp_at.reshape(1)
    lat = jnp.pad(latent.reshape(rows, 4 * LAT_CH), ((0, 0), (SIDE, SIDE)))
    tail = jnp.transpose(frame_tail, (1, 0, 2, 3, 4)).reshape(videos * tail_frames, -1)
    own, above, below = edges(grp_at, tail, lat)

    taps = spread_taps(conv_weight)
    w = lax.dynamic_slice_in_dim(head_weight, seq_at[0] * HD, HD, axis=0)
    w = jnp.concatenate([w[:, SIDE:], w, w[:, :SIDE]], axis=1)
    gain = jnp.tile(latent_scale, HD // LAT_CH).reshape(1, HD)
    shift = jnp.tile(latent_shift, HD // LAT_CH).reshape(1, HD)

    sigma = jnp.broadcast_to(sigma.reshape(1, 1), (1, HD))
    bias = conv_bias.reshape(1, -1)
    mine, w, lat, own, above, below, taps, gain, shift, bias, sigma = lax.optimization_barrier(
        (mine, w, lat, own, above, below, taps, gain, shift, bias, sigma)
    )

    parts = lax.all_to_all(attend(mine, w), "seq", 0, 0, tiled=True)
    bands_out = update(seq_at, parts, lat, above, below, sigma, gain, shift, features, bands)
    tiles = lax.all_to_all(bands_out, "grp", 0, 0, tiled=True)
    return convolve(grp_at, tiles, own, above, below, taps, bias)


def solution(mesh):
    return jax.shard_map(
        on_device,
        mesh=mesh,
        in_specs=(
            P("grp", "seq", None, None, None),
            P("grp", "seq", None, None, None),
            P("grp", "seq", None, None, None),
            P("grp", "seq", None, None, None),
            P("grp"),
            P(),
            P(),
            P(),
            P(None, None, "seq", "grp", None),
            P(),
            P(),
        ),
        out_specs=P(None, None, "seq", "grp", None),
        check_vma=False,
    )
```

```python
import functools
import math

import jax
import jax.numpy as jnp
import numpy as np
from jax import lax
from jax.experimental import pallas as pl
from jax.experimental.pallas import tpu as pltpu
from jax.sharding import PartitionSpec as P

HD = 128
LAT_CH = 16
NORM_EPS = 1e-06
F32 = jnp.float32
BF16 = jnp.bfloat16
VMEM = pltpu.VMEM
SIDE = 2 * LAT_CH


def dot_nt(a, b):
    return lax.dot_general(a, b, (((1,), (1,)), ((), ())), preferred_element_type=F32)


def dot_nn(a, b):
    return jnp.dot(a, b, preferred_element_type=F32)


def pack_kernel(q_ref, k_ref, v_ref, o_ref):
    rows = q_ref.shape[0]
    for place, ref in enumerate((q_ref, k_ref, v_ref)):
        for head in range(o_ref.shape[0]):
            o_ref[head, place * rows : (place + 1) * rows, :] = ref[:, head * HD : (head + 1) * HD]


def pack_heads(query, keys, values, heads, steps=2):
    rows, features = query.shape
    width = features // steps
    spec = pl.BlockSpec((rows, width), lambda i: (0, i))
    return pl.pallas_call(
        pack_kernel,
        grid=(steps,),
        in_specs=[spec] * 3,
        out_specs=pl.BlockSpec((heads // steps, 3 * rows, HD), lambda i: (i, 0, 0)),
        out_shape=jax.ShapeDtypeStruct((heads, 3 * rows, HD), BF16),
        name="pack_heads",
    )(query, keys, values)


def attend_kernel(
    block_tr, x_ref, w_ref, o_ref, queries, keys, kk, vx, held, vel, ssq, sems, *buffers
):
    tr, rows3, _ = x_ref.shape
    rows = rows3 // 3
    into = (queries, keys, vx.at[:, :, :HD])
    fetches = [
        pltpu.make_async_copy(x_ref.at[:, n * rows : (n + 1) * rows, :], into[n], sems.at[n])
        for n in range(3)
    ]
    for n in (1, 0, 2):
        fetches[n].start()
    tokens, block = tr * rows, block_tr * rows
    steps = tr // block_tr
    factor = math.log2(math.e) / math.sqrt(HD)
    chunk_tr = 8
    chunk = chunk_tr * rows

    def score(step):
        s_ref, peak_ref = buffers[step % 2], buffers[2 + step % 2]
        q = queries[step * block_tr : (step + 1) * block_tr].reshape(block, HD)
        q = q.astype(F32) * factor
        high = q.astype(BF16)
        q = jnp.concatenate([high, (q - high.astype(F32)).astype(BF16)], axis=1)
        peak = None
        for c in range(tr // chunk_tr):
            at = slice(c * chunk, (c + 1) * chunk)
            if step == 0:
                piece = keys[c * chunk_tr : (c + 1) * chunk_tr]
                flipped = piece.reshape(chunk, HD).astype(F32).T.astype(BF16)
                kk[:HD, at] = flipped
                kk[HD:, at] = flipped
            s = dot_nn(q, kk[:, at])
            s_ref[:, at] = s
            for l in range(0, chunk, HD):
                part = s[:, l : l + HD]
                peak = part if peak is None else jnp.maximum(peak, part)
        peak_ref[...] = jnp.broadcast_to(jnp.max(peak, axis=1, keepdims=True), peak_ref.shape)

    def mix(step):
        s_ref, peak_ref = buffers[step % 2], buffers[2 + step % 2]
        peak = peak_ref[...]
        weights = jnp.concatenate(
            [
                jnp.exp2(s_ref[:, l : l + HD] - peak).astype(BF16)
                for l in range(0, tokens, HD)
            ],
            axis=1,
        )
        mixed = dot_nn(weights, vx[...].reshape(tokens, 2 * HD))
        held[step * block : (step + 1) * block, :] = (mixed[:, :HD] / mixed[:, HD:]).astype(BF16)

    lane = lax.broadcasted_iota(jnp.int32, (rows, HD), 1)
    line = lax.broadcasted_iota(jnp.int32, (16, HD), 0)

    def send(r):
        up, down = (r - 1) % tr, (r + 1) % tr
        piece = [vel[t * rows : (t + 1) * rows, :] for t in (up, r, down)]
        merged = jnp.where(lane < SIDE, piece[0], jnp.where(lane < 3 * SIDE, piece[1], piece[2]))
        o_ref[r, :rows, :] = merged.astype(BF16)
        merged = jnp.where(line == 0, ssq[up], jnp.where(line == 1, ssq[r], ssq[down]))
        o_ref[r, rows:, :] = merged.astype(BF16)

    ssq[...] = jnp.zeros_like(ssq)
    fetches[1].wait()
    fetches[0].wait()
    score(0)
    fetches[2].wait()
    vx[:, :, HD:] = jnp.ones((tr, rows, HD), BF16)
    for step in range(steps):
        if step + 1 < steps:
            score(step + 1)
        mix(step)
    vel[...] = dot_nn(held[...], w_ref[...])
    wide = held[...].astype(F32)
    total = dot_nt(jnp.ones((16, HD), BF16), (wide * wide).astype(BF16))
    for r in range(tr):
        ssq[r, :, :rows] = total[:, r * rows : (r + 1) * rows]
    for r in range(tr):
        send(r)


def attend(x, w, block_tr=4):
    tr, rows3, _ = x.shape
    rows = rows3 // 3
    tokens, block = tr * rows, block_tr * rows
    return pl.pallas_call(
        functools.partial(attend_kernel, block_tr),
        in_specs=[pl.BlockSpec(memory_space=pl.ANY), pl.BlockSpec(memory_space=VMEM)],
        out_specs=pl.BlockSpec(memory_space=VMEM),
        out_shape=jax.ShapeDtypeStruct((tr, rows + 16, HD), BF16),
        scratch_shapes=[
            VMEM((tr, rows, HD), BF16),
            VMEM((tr, rows, HD), BF16),
            VMEM((2 * HD, tokens), BF16),
            VMEM((tr, rows, 2 * HD), BF16),
            VMEM((tokens, HD), BF16),
            VMEM((tokens, HD), F32),
            VMEM((tr, 16, HD), F32),
            pltpu.SemaphoreType.DMA((3,)),
            VMEM((block, tokens), F32),
            VMEM((block, tokens), F32),
            VMEM((block, HD), F32),
            VMEM((block, HD), F32),
        ],
        compiler_params=pltpu.CompilerParams(vmem_limit_bytes=32 << 20),
        cost_estimate=pl.CostEstimate(
            flops=8 * tokens * tokens * HD, bytes_accessed=4 << 20, transcendentals=tokens * tokens
        ),
        name="attend",
    )(x, w)


def update_kernel(
    features, bands, index_ref, y_ref, lat_ref, above_ref, below_ref, sigma_ref, gain_ref, shift_ref, o_ref
):
    heads, lines, _ = y_ref.shape
    rows = lines - 16
    frames = 4
    cols = rows // frames
    total = y_ref[0].astype(F32)
    for h in range(1, heads):
        total = total + y_ref[h].astype(F32)
    velocity = total[:rows]
    sums = jnp.concatenate([total[rows:], jnp.zeros((HD - 16, HD), F32)], axis=0).T
    lane = lax.broadcasted_iota(jnp.int32, (rows, HD), 1)
    up, own, down = (jnp.broadcast_to(sums[:rows, i : i + 1], (rows, HD)) for i in range(3))
    square = jnp.where(lane < SIDE, up, jnp.where(lane < 3 * SIDE, own, down))
    velocity = velocity / jnp.sqrt(square * (1.0 / features) + NORM_EPS)
    above = above_ref[...].astype(F32)
    below = below_ref[...].astype(F32)
    above = above + pltpu.roll(above, HD - SIDE, 1) + pltpu.roll(above, HD - 2 * SIDE, 1)
    below = pltpu.roll(below, 3 * SIDE, 1) + pltpu.roll(below, 2 * SIDE, 1) + pltpu.roll(below, SIDE, 1)
    lat = jnp.where(lane < SIDE, above, jnp.where(lane < 3 * SIDE, lat_ref[...], below))
    cleaned = lat - sigma_ref[...] * velocity
    scaled = cleaned * gain_ref[...] + shift_ref[...]
    first, last = index_ref[0] == 0, index_ref[0] == heads - 1
    drop = ((lane < SIDE) & first) | ((lane >= 3 * SIDE) & last)
    scaled = jnp.where(drop, 0.0, scaled).astype(BF16)
    count = bands * 4 * frames
    at = lax.broadcasted_iota(jnp.int32, (count, rows), 0)
    source = lax.broadcasted_iota(jnp.int32, (count, rows), 1)
    band, frame, t = at // (4 * frames), (at // 4) % frames, at % 4
    column = (3 * band + 1) // 2 - 1 + t
    hit = (source == frame * cols + column) & (column >= 0) & (column < cols)
    chosen = jnp.where(hit, 1.0, 0.0).astype(BF16)
    o_ref[...] = dot_nn(chosen, scaled).astype(BF16).reshape(o_ref.shape)


def update(index, y, lat, above, below, sigma, gain, shift, features, bands):
    smem = pl.BlockSpec(memory_space=pltpu.SMEM)
    vmem = pl.BlockSpec(memory_space=VMEM)
    return pl.pallas_call(
        functools.partial(update_kernel, features, bands),
        in_specs=[smem] + [vmem] * 7,
        out_specs=vmem,
        out_shape=jax.ShapeDtypeStruct((bands, 16, HD), BF16),
        compiler_params=pltpu.CompilerParams(vmem_limit_bytes=16 << 20),
        name="update",
    )(index, y, lat, above, below, sigma, gain, shift)


def columns_kernel(index_ref, tail_ref, own_ref, right_ref, left_ref):
    count, width = tail_ref.shape
    odd = index_ref[0] % 2
    shape = (width, 3 * HD)
    k = lax.broadcasted_iota(jnp.int32, shape, 0)
    n = lax.broadcasted_iota(jnp.int32, shape, 1)
    pixel = k // LAT_CH
    i = jnp.where(pixel >= 3, 1, 0)
    j = pixel - 3 * i
    same = ((k % LAT_CH) == (n % LAT_CH)) & ((n % HD) // SIDE == i + 1)
    slot = 2 * (n // HD) + (n % SIDE) // LAT_CH
    for dz, out_ref in ((0, own_ref), (1, right_ref), (-1, left_ref)):
        shift = 1 - odd if dz == 0 else odd
        hit = same & (slot == j + (1 - 3 * dz) + shift)
        if dz:
            hit = hit & (j == (2 if dz == 1 else 0))
        placed = dot_nn(tail_ref[...], jnp.where(hit, 1.0, 0.0).astype(BF16)).astype(BF16)
        for t in range(3):
            out_ref[t * count : (t + 1) * count, :] = placed[:, t * HD : (t + 1) * HD]


def rows_kernel(own_ref, before_ref, after_ref, lat_ref, tile_ref, down_ref, up_ref):
    tile = own_ref[...].astype(F32) + before_ref[...].astype(F32) + after_ref[...].astype(F32)
    tile_ref[...] = tile.astype(BF16)
    lat = lat_ref[...]
    high = lat.astype(BF16).astype(F32)
    rest = lat - high
    mid = rest.astype(BF16).astype(F32)
    low = rest - mid
    lane = lax.broadcasted_iota(jnp.int32, lat.shape, 1)
    for out_ref, start in ((down_ref, 2 * SIDE), (up_ref, SIDE)):
        parts = []
        for place, part in enumerate((high, mid, low, tile)):
            turn = (place * SIDE - start) % HD
            parts.append(pltpu.roll(part, turn, 1) if turn else part)
        merged = jnp.where(lane < 3 * SIDE, parts[2], parts[3])
        merged = jnp.where(lane < SIDE, parts[0], jnp.where(lane < 2 * SIDE, parts[1], merged))
        out_ref[...] = merged.astype(BF16)


def edges(index, tail, lat):
    assert lat.shape[0] == 3 * tail.shape[0]
    vmem = pl.BlockSpec(memory_space=VMEM)
    tile = jax.ShapeDtypeStruct(lat.shape, BF16)
    small = pltpu.CompilerParams(vmem_limit_bytes=8 << 20)
    own, right, left = pl.pallas_call(
        columns_kernel,
        in_specs=[pl.BlockSpec(memory_space=pltpu.SMEM), vmem],
        out_specs=[vmem] * 3,
        out_shape=[tile] * 3,
        compiler_params=small,
        name="edge_columns",
    )(index, tail)
    before, after = to_next(right, "grp"), to_last(left, "grp")
    own, down, up = pl.pallas_call(
        rows_kernel,
        in_specs=[vmem] * 4,
        out_specs=[vmem] * 3,
        out_shape=[tile] * 3,
        compiler_params=small,
        name="edge_rows",
    )(own, before, after, lat)
    return own, to_next(down, "seq"), to_last(up, "seq")


def to_next(array, axis):
    return lax.ppermute(array, axis, [(i, i + 1) for i in range(lax.axis_size(axis) - 1)])


def to_last(array, axis):
    return lax.ppermute(array, axis, [(i + 1, i) for i in range(lax.axis_size(axis) - 1)])


STARTS = (((0, 1), (1, 0), (1, 1)), ((0, 0), (0, 1), (1, 0)))


def taps_kernel(w_ref, o_ref):
    out = w_ref.shape[1]
    o_ref[...] = jnp.zeros_like(o_ref)
    for kind, start in enumerate(STARTS):
        for tf in range(3):
            for ti in range(3):
                for tj, (token, b) in enumerate(start):
                    tap = ((tf * 3 + ti) * 3 + tj) * LAT_CH
                    piece = w_ref[tap : tap + LAT_CH, :]
                    for i in range(2):
                        at = tf * 2 * HD + token * HD + (i + ti) * SIDE + b * LAT_CH
                        o_ref[kind, at : at + LAT_CH, i * out : (i + 1) * out] = piece


def spread_taps(conv_weight):
    out = conv_weight.shape[1]
    return pl.pallas_call(
        taps_kernel,
        in_specs=[pl.BlockSpec(memory_space=VMEM)],
        out_specs=pl.BlockSpec(memory_space=VMEM),
        out_shape=jax.ShapeDtypeStruct((2, 6 * HD, 2 * out), BF16),
        compiler_params=pltpu.CompilerParams(vmem_limit_bytes=8 << 20),
        name="spread_taps",
    )(conv_weight)


def conv_kernel(index_ref, z_ref, own_ref, above_ref, below_ref, taps_ref, bias_ref, o_ref):
    videos, lines, _ = z_ref.shape
    frames = lines // 4
    out = bias_ref.shape[1]
    odd = index_ref[0] % 2
    count = videos * frames
    at = lax.broadcasted_iota(jnp.int32, (3 * count, videos * lines), 0)
    source = lax.broadcasted_iota(jnp.int32, (3 * count, videos * lines), 1)
    t, frame, video = at // count, (at // videos) % frames, at % videos
    chosen = jnp.where(source == video * lines + frame * 4 + t, 1.0, 0.0).astype(BF16)
    image = dot_nn(chosen, z_ref[...].reshape(videos * lines, HD)).astype(BF16)
    above = pltpu.roll(above_ref[...].astype(F32), SIDE, 1)
    cached = own_ref[...].astype(F32)
    lane = lax.broadcasted_iota(jnp.int32, cached.shape, 1)
    cached = jnp.where(lane < 3 * SIDE, cached, below_ref[...].astype(F32))
    cached = jnp.where(lane < SIDE, above, cached).astype(BF16)
    held = cached.shape[0] // 3
    token = [
        jnp.concatenate(
            [cached[t * held : (t + 1) * held], image[t * count : (t + 1) * count]], axis=0
        )
        for t in range(3)
    ]

    def windows(first, second):
        wide = jnp.concatenate([first, second], axis=1)
        return jnp.concatenate([wide[tf * videos : tf * videos + count] for tf in range(3)], axis=1)

    middle = jnp.where(odd == 1, windows(token[0], token[1]), windows(token[1], token[2]))
    outer = jnp.concatenate([windows(token[0], token[1]), windows(token[1], token[2])], axis=0)
    outer = dot_nn(outer, taps_ref[odd])
    inner = dot_nn(middle, taps_ref[1 - odd])
    for j, part in enumerate((outer[:count], inner, outer[count:])):
        done = []
        for i in range(2):
            conv = part[:, i * out : (i + 1) * out] + bias_ref[...]
            mean_sq = jnp.mean(conv * conv, axis=1, keepdims=True)
            normed = conv / jnp.sqrt(mean_sq + NORM_EPS)
            done.append(normed / (1.0 + jnp.exp(-normed)))
        for f in range(frames):
            at = slice(f * videos, (f + 1) * videos)
            tile = jnp.concatenate([d[at][:, None, :] for d in done], axis=1)
            o_ref[:, f, j] = tile.astype(BF16)


def convolve(index, z, own, above, below, taps, bias):
    videos, lines, _ = z.shape
    out = bias.shape[1]
    vmem = pl.BlockSpec(memory_space=VMEM)
    return pl.pallas_call(
        conv_kernel,
        in_specs=[pl.BlockSpec(memory_space=pltpu.SMEM)] + [vmem] * 6,
        out_specs=vmem,
        out_shape=jax.ShapeDtypeStruct((videos, lines // 4, 3, 2, out), BF16),
        compiler_params=pltpu.CompilerParams(vmem_limit_bytes=16 << 20),
        name="convolve",
    )(index, z, own, above, below, taps, bias).transpose(0, 1, 3, 2, 4)


def on_device(
    query,
    key_states,
    value_states,
    latent,
    sigma,
    head_weight,
    latent_scale,
    latent_shift,
    frame_tail,
    conv_weight,
    conv_bias,
):
    features = query.shape[4]
    heads = features // HD
    frames, cols = latent.shape[2], latent.shape[3]
    rows = frames * cols
    bands = lax.axis_size("grp")
    seq_at, grp_at = lax.axis_index("seq"), lax.axis_index("grp")
    videos, tail_frames = frame_tail.shape[0], frame_tail.shape[1]

    sent = pack_heads(
        query.reshape(rows, features),
        key_states.reshape(rows, features),
        value_states.reshape(rows, features),
        heads,
    )
    mine = lax.all_to_all(sent, "seq", 0, 0, tiled=True)

    seq_at, grp_at = seq_at.reshape(1), grp_at.reshape(1)
    lat = jnp.pad(latent.reshape(rows, 4 * LAT_CH), ((0, 0), (SIDE, SIDE)))
    tail = jnp.transpose(frame_tail, (1, 0, 2, 3, 4)).reshape(videos * tail_frames, -1)
    own, above, below = edges(grp_at, tail, lat)

    taps = spread_taps(conv_weight)
    w = lax.dynamic_slice_in_dim(head_weight, seq_at[0] * HD, HD, axis=0)
    w = jnp.concatenate([w[:, SIDE:], w, w[:, :SIDE]], axis=1)
    gain = jnp.tile(latent_scale, HD // LAT_CH).reshape(1, HD)
    shift = jnp.tile(latent_shift, HD // LAT_CH).reshape(1, HD)

    sigma = jnp.broadcast_to(sigma.reshape(1, 1), (1, HD))
    bias = conv_bias.reshape(1, -1)
    mine, w, lat, own, above, below, taps, gain, shift, bias, sigma = lax.optimization_barrier(
        (mine, w, lat, own, above, below, taps, gain, shift, bias, sigma)
    )

    parts = lax.all_to_all(attend(mine, w), "seq", 0, 0, tiled=True)
    bands_out = update(seq_at, parts, lat, above, below, sigma, gain, shift, features, bands)
    tiles = lax.all_to_all(bands_out, "grp", 0, 0, tiled=True)
    return convolve(grp_at, tiles, own, above, below, taps, bias)


def solution(mesh):
    return jax.shard_map(
        on_device,
        mesh=mesh,
        in_specs=(
            P("grp", "seq", None, None, None),
            P("grp", "seq", None, None, None),
            P("grp", "seq", None, None, None),
            P("grp", "seq", None, None, None),
            P("grp"),
            P(),
            P(),
            P(),
            P(None, None, "seq", "grp", None),
            P(),
            P(),
        ),
        out_specs=P(None, None, "seq", "grp", None),
        check_vma=False,
    )
```

```python
import functools
import math

import jax
import jax.numpy as jnp
import numpy as np
from jax import lax
from jax.experimental import pallas as pl
from jax.experimental.pallas import tpu as pltpu
from jax.sharding import PartitionSpec as P

HD = 128
LAT_CH = 16
NORM_EPS = 1e-06
F32 = jnp.float32
BF16 = jnp.bfloat16
VMEM = pltpu.VMEM
SIDE = 2 * LAT_CH


def dot_nt(a, b):
    return lax.dot_general(a, b, (((1,), (1,)), ((), ())), preferred_element_type=F32)


def dot_nn(a, b):
    return jnp.dot(a, b, preferred_element_type=F32)


def pack_kernel(q_ref, k_ref, v_ref, o_ref):
    rows = q_ref.shape[0]
    for place, ref in enumerate((q_ref, k_ref, v_ref)):
        for head in range(o_ref.shape[0]):
            o_ref[head, place * rows : (place + 1) * rows, :] = ref[:, head * HD : (head + 1) * HD]


def pack_heads(query, keys, values, heads, steps=2):
    rows, features = query.shape
    width = features // steps
    spec = pl.BlockSpec((rows, width), lambda i: (0, i))
    return pl.pallas_call(
        pack_kernel,
        grid=(steps,),
        in_specs=[spec] * 3,
        out_specs=pl.BlockSpec((heads // steps, 3 * rows, HD), lambda i: (i, 0, 0)),
        out_shape=jax.ShapeDtypeStruct((heads, 3 * rows, HD), BF16),
        name="pack_heads",
    )(query, keys, values)


def attend_kernel(
    block_tr, x_ref, w_ref, o_ref, queries, keys, kk, vx, held, vel, ssq, sems, *buffers
):
    tr, rows3, _ = x_ref.shape
    rows = rows3 // 3
    into = (queries, keys, vx.at[:, :, :HD])
    fetches = [
        pltpu.make_async_copy(x_ref.at[:, n * rows : (n + 1) * rows, :], into[n], sems.at[n])
        for n in range(3)
    ]
    for n in (1, 0, 2):
        fetches[n].start()
    tokens, block = tr * rows, block_tr * rows
    steps = tr // block_tr
    factor = math.log2(math.e) / math.sqrt(HD)
    chunk_tr = 8
    chunk = chunk_tr * rows

    def score(step):
        s_ref, peak_ref = buffers[step % 2], buffers[2 + step % 2]
        q = queries[step * block_tr : (step + 1) * block_tr].reshape(block, HD)
        q = q.astype(F32) * factor
        high = q.astype(BF16)
        q = jnp.concatenate([high, (q - high.astype(F32)).astype(BF16)], axis=1)
        peak = None
        for c in range(tr // chunk_tr):
            at = slice(c * chunk, (c + 1) * chunk)
            if step == 0:
                piece = keys[c * chunk_tr : (c + 1) * chunk_tr]
                flipped = piece.reshape(chunk, HD).astype(F32).T.astype(BF16)
                kk[:HD, at] = flipped
                kk[HD:, at] = flipped
            s = dot_nn(q, kk[:, at])
            s_ref[:, at] = s
            for l in range(0, chunk, HD):
                part = s[:, l : l + HD]
                peak = part if peak is None else jnp.maximum(peak, part)
        peak_ref[...] = jnp.broadcast_to(jnp.max(peak, axis=1, keepdims=True), peak_ref.shape)

    def mix(step):
        s_ref, peak_ref = buffers[step % 2], buffers[2 + step % 2]
        peak = peak_ref[...]
        weights = jnp.concatenate(
            [
                jnp.exp2(s_ref[:, l : l + HD] - peak).astype(BF16)
                for l in range(0, tokens, HD)
            ],
            axis=1,
        )
        mixed = dot_nn(weights, vx[...].reshape(tokens, 2 * HD))
        held[step * block : (step + 1) * block, :] = (mixed[:, :HD] / mixed[:, HD:]).astype(BF16)

    lane = lax.broadcasted_iota(jnp.int32, (rows, HD), 1)
    line = lax.broadcasted_iota(jnp.int32, (16, HD), 0)

    def send(r):
        up, down = (r - 1) % tr, (r + 1) % tr
        piece = [vel[t * rows : (t + 1) * rows, :] for t in (up, r, down)]
        merged = jnp.where(lane < SIDE, piece[0], jnp.where(lane < 3 * SIDE, piece[1], piece[2]))
        o_ref[r, :rows, :] = merged.astype(BF16)
        merged = jnp.where(line == 0, ssq[up], jnp.where(line == 1, ssq[r], ssq[down]))
        o_ref[r, rows:, :] = merged.astype(BF16)

    ssq[...] = jnp.zeros_like(ssq)
    fetches[1].wait()
    fetches[0].wait()
    score(0)
    fetches[2].wait()
    vx[:, :, HD:] = jnp.ones((tr, rows, HD), BF16)
    for step in range(steps):
        if step + 1 < steps:
            score(step + 1)
        mix(step)
    vel[...] = dot_nn(held[...], w_ref[...])
    wide = held[...].astype(F32)
    total = dot_nt(jnp.ones((16, HD), BF16), (wide * wide).astype(BF16))
    for r in range(tr):
        ssq[r, :, :rows] = total[:, r * rows : (r + 1) * rows]
    for r in range(tr):
        send(r)


def attend(x, w, block_tr=4):
    tr, rows3, _ = x.shape
    rows = rows3 // 3
    tokens, block = tr * rows, block_tr * rows
    return pl.pallas_call(
        functools.partial(attend_kernel, block_tr),
        in_specs=[pl.BlockSpec(memory_space=pl.ANY), pl.BlockSpec(memory_space=VMEM)],
        out_specs=pl.BlockSpec(memory_space=VMEM),
        out_shape=jax.ShapeDtypeStruct((tr, rows + 16, HD), BF16),
        scratch_shapes=[
            VMEM((tr, rows, HD), BF16),
            VMEM((tr, rows, HD), BF16),
            VMEM((2 * HD, tokens), BF16),
            VMEM((tr, rows, 2 * HD), BF16),
            VMEM((tokens, HD), BF16),
            VMEM((tokens, HD), F32),
            VMEM((tr, 16, HD), F32),
            pltpu.SemaphoreType.DMA((3,)),
            VMEM((block, tokens), F32),
            VMEM((block, tokens), F32),
            VMEM((block, HD), F32),
            VMEM((block, HD), F32),
        ],
        compiler_params=pltpu.CompilerParams(vmem_limit_bytes=32 << 20),
        cost_estimate=pl.CostEstimate(
            flops=8 * tokens * tokens * HD, bytes_accessed=4 << 20, transcendentals=tokens * tokens
        ),
        name="attend",
    )(x, w)


def update_kernel(
    features, bands, index_ref, y_ref, lat_ref, above_ref, below_ref, sigma_ref, gain_ref, shift_ref, o_ref
):
    heads, lines, _ = y_ref.shape
    rows = lines - 16
    frames = 4
    cols = rows // frames
    total = y_ref[0].astype(F32)
    for h in range(1, heads):
        total = total + y_ref[h].astype(F32)
    velocity = total[:rows]
    sums = jnp.concatenate([total[rows:], jnp.zeros((HD - 16, HD), F32)], axis=0).T
    lane = lax.broadcasted_iota(jnp.int32, (rows, HD), 1)
    up, own, down = (jnp.broadcast_to(sums[:rows, i : i + 1], (rows, HD)) for i in range(3))
    square = jnp.where(lane < SIDE, up, jnp.where(lane < 3 * SIDE, own, down))
    velocity = velocity * lax.rsqrt(square * (1.0 / features) + NORM_EPS)
    above = above_ref[...].astype(F32)
    below = below_ref[...].astype(F32)
    above = above + pltpu.roll(above, HD - SIDE, 1) + pltpu.roll(above, HD - 2 * SIDE, 1)
    below = pltpu.roll(below, 3 * SIDE, 1) + pltpu.roll(below, 2 * SIDE, 1) + pltpu.roll(below, SIDE, 1)
    lat = jnp.where(lane < SIDE, above, jnp.where(lane < 3 * SIDE, lat_ref[...], below))
    cleaned = lat - sigma_ref[...] * velocity
    scaled = cleaned * gain_ref[...] + shift_ref[...]
    first, last = index_ref[0] == 0, index_ref[0] == heads - 1
    drop = ((lane < SIDE) & first) | ((lane >= 3 * SIDE) & last)
    scaled = jnp.where(drop, 0.0, scaled).astype(BF16)
    count = bands * 4 * frames
    at = lax.broadcasted_iota(jnp.int32, (count, rows), 0)
    source = lax.broadcasted_iota(jnp.int32, (count, rows), 1)
    band, frame, t = at // (4 * frames), (at // 4) % frames, at % 4
    column = (3 * band + 1) // 2 - 1 + t
    hit = (source == frame * cols + column) & (column >= 0) & (column < cols)
    chosen = jnp.where(hit, 1.0, 0.0).astype(BF16)
    o_ref[...] = dot_nn(chosen, scaled).astype(BF16).reshape(o_ref.shape)


def update(index, y, lat, above, below, sigma, gain, shift, features, bands):
    smem = pl.BlockSpec(memory_space=pltpu.SMEM)
    vmem = pl.BlockSpec(memory_space=VMEM)
    return pl.pallas_call(
        functools.partial(update_kernel, features, bands),
        in_specs=[smem] + [vmem] * 7,
        out_specs=vmem,
        out_shape=jax.ShapeDtypeStruct((bands, 16, HD), BF16),
        compiler_params=pltpu.CompilerParams(vmem_limit_bytes=16 << 20),
        name="update",
    )(index, y, lat, above, below, sigma, gain, shift)


def columns_kernel(index_ref, tail_ref, own_ref, right_ref, left_ref):
    count, width = tail_ref.shape
    odd = index_ref[0] % 2
    shape = (width, 3 * HD)
    k = lax.broadcasted_iota(jnp.int32, shape, 0)
    n = lax.broadcasted_iota(jnp.int32, shape, 1)
    pixel = k // LAT_CH
    i = jnp.where(pixel >= 3, 1, 0)
    j = pixel - 3 * i
    same = ((k % LAT_CH) == (n % LAT_CH)) & ((n % HD) // SIDE == i + 1)
    slot = 2 * (n // HD) + (n % SIDE) // LAT_CH
    for dz, out_ref in ((0, own_ref), (1, right_ref), (-1, left_ref)):
        shift = 1 - odd if dz == 0 else odd
        hit = same & (slot == j + (1 - 3 * dz) + shift)
        if dz:
            hit = hit & (j == (2 if dz == 1 else 0))
        placed = dot_nn(tail_ref[...], jnp.where(hit, 1.0, 0.0).astype(BF16)).astype(BF16)
        for t in range(3):
            out_ref[t * count : (t + 1) * count, :] = placed[:, t * HD : (t + 1) * HD]


def rows_kernel(own_ref, before_ref, after_ref, lat_ref, tile_ref, down_ref, up_ref):
    tile = own_ref[...].astype(F32) + before_ref[...].astype(F32) + after_ref[...].astype(F32)
    tile_ref[...] = tile.astype(BF16)
    lat = lat_ref[...]
    high = lat.astype(BF16).astype(F32)
    rest = lat - high
    mid = rest.astype(BF16).astype(F32)
    low = rest - mid
    lane = lax.broadcasted_iota(jnp.int32, lat.shape, 1)
    for out_ref, start in ((down_ref, 2 * SIDE), (up_ref, SIDE)):
        parts = []
        for place, part in enumerate((high, mid, low, tile)):
            turn = (place * SIDE - start) % HD
            parts.append(pltpu.roll(part, turn, 1) if turn else part)
        merged = jnp.where(lane < 3 * SIDE, parts[2], parts[3])
        merged = jnp.where(lane < SIDE, parts[0], jnp.where(lane < 2 * SIDE, parts[1], merged))
        out_ref[...] = merged.astype(BF16)


def edges(index, tail, lat):
    assert lat.shape[0] == 3 * tail.shape[0]
    vmem = pl.BlockSpec(memory_space=VMEM)
    tile = jax.ShapeDtypeStruct(lat.shape, BF16)
    small = pltpu.CompilerParams(vmem_limit_bytes=8 << 20)
    own, right, left = pl.pallas_call(
        columns_kernel,
        in_specs=[pl.BlockSpec(memory_space=pltpu.SMEM), vmem],
        out_specs=[vmem] * 3,
        out_shape=[tile] * 3,
        compiler_params=small,
        name="edge_columns",
    )(index, tail)
    before, after = to_next(right, "grp"), to_last(left, "grp")
    own, down, up = pl.pallas_call(
        rows_kernel,
        in_specs=[vmem] * 4,
        out_specs=[vmem] * 3,
        out_shape=[tile] * 3,
        compiler_params=small,
        name="edge_rows",
    )(own, before, after, lat)
    return own, to_next(down, "seq"), to_last(up, "seq")


def to_next(array, axis):
    return lax.ppermute(array, axis, [(i, i + 1) for i in range(lax.axis_size(axis) - 1)])


def to_last(array, axis):
    return lax.ppermute(array, axis, [(i + 1, i) for i in range(lax.axis_size(axis) - 1)])


STARTS = (((0, 1), (1, 0), (1, 1)), ((0, 0), (0, 1), (1, 0)))


def taps_kernel(w_ref, o_ref):
    out = w_ref.shape[1]
    o_ref[...] = jnp.zeros_like(o_ref)
    for kind, start in enumerate(STARTS):
        for tf in range(3):
            for ti in range(3):
                for tj, (token, b) in enumerate(start):
                    tap = ((tf * 3 + ti) * 3 + tj) * LAT_CH
                    piece = w_ref[tap : tap + LAT_CH, :]
                    for i in range(2):
                        at = tf * 2 * HD + token * HD + (i + ti) * SIDE + b * LAT_CH
                        o_ref[kind, at : at + LAT_CH, i * out : (i + 1) * out] = piece


def spread_taps(conv_weight):
    out = conv_weight.shape[1]
    return pl.pallas_call(
        taps_kernel,
        in_specs=[pl.BlockSpec(memory_space=VMEM)],
        out_specs=pl.BlockSpec(memory_space=VMEM),
        out_shape=jax.ShapeDtypeStruct((2, 6 * HD, 2 * out), BF16),
        compiler_params=pltpu.CompilerParams(vmem_limit_bytes=8 << 20),
        name="spread_taps",
    )(conv_weight)


def conv_kernel(index_ref, z_ref, own_ref, above_ref, below_ref, taps_ref, bias_ref, o_ref):
    videos, lines, _ = z_ref.shape
    frames = lines // 4
    out = bias_ref.shape[1]
    odd = index_ref[0] % 2
    count = videos * frames
    at = lax.broadcasted_iota(jnp.int32, (3 * count, videos * lines), 0)
    source = lax.broadcasted_iota(jnp.int32, (3 * count, videos * lines), 1)
    t, frame, video = at // count, (at // videos) % frames, at % videos
    chosen = jnp.where(source == video * lines + frame * 4 + t, 1.0, 0.0).astype(BF16)
    image = dot_nn(chosen, z_ref[...].reshape(videos * lines, HD)).astype(BF16)
    above = pltpu.roll(above_ref[...].astype(F32), SIDE, 1)
    cached = own_ref[...].astype(F32)
    lane = lax.broadcasted_iota(jnp.int32, cached.shape, 1)
    cached = jnp.where(lane < 3 * SIDE, cached, below_ref[...].astype(F32))
    cached = jnp.where(lane < SIDE, above, cached).astype(BF16)
    held = cached.shape[0] // 3
    token = [
        jnp.concatenate(
            [cached[t * held : (t + 1) * held], image[t * count : (t + 1) * count]], axis=0
        )
        for t in range(3)
    ]

    def windows(first, second):
        wide = jnp.concatenate([first, second], axis=1)
        return jnp.concatenate([wide[tf * videos : tf * videos + count] for tf in range(3)], axis=1)

    middle = jnp.where(odd == 1, windows(token[0], token[1]), windows(token[1], token[2]))
    outer = jnp.concatenate([windows(token[0], token[1]), windows(token[1], token[2])], axis=0)
    outer = dot_nn(outer, taps_ref[odd])
    inner = dot_nn(middle, taps_ref[1 - odd])
    for j, part in enumerate((outer[:count], inner, outer[count:])):
        done = []
        for i in range(2):
            conv = part[:, i * out : (i + 1) * out] + bias_ref[...]
            mean_sq = jnp.mean(conv * conv, axis=1, keepdims=True)
            normed = conv * lax.rsqrt(mean_sq + NORM_EPS)
            done.append(normed / (1.0 + jnp.exp(-normed)))
        for f in range(frames):
            at = slice(f * videos, (f + 1) * videos)
            tile = jnp.concatenate([d[at][:, None, :] for d in done], axis=1)
            o_ref[:, f, j] = tile.astype(BF16)


def convolve(index, z, own, above, below, taps, bias):
    videos, lines, _ = z.shape
    out = bias.shape[1]
    vmem = pl.BlockSpec(memory_space=VMEM)
    return pl.pallas_call(
        conv_kernel,
        in_specs=[pl.BlockSpec(memory_space=pltpu.SMEM)] + [vmem] * 6,
        out_specs=vmem,
        out_shape=jax.ShapeDtypeStruct((videos, lines // 4, 3, 2, out), BF16),
        compiler_params=pltpu.CompilerParams(vmem_limit_bytes=16 << 20),
        name="convolve",
    )(index, z, own, above, below, taps, bias).transpose(0, 1, 3, 2, 4)


def on_device(
    query,
    key_states,
    value_states,
    latent,
    sigma,
    head_weight,
    latent_scale,
    latent_shift,
    frame_tail,
    conv_weight,
    conv_bias,
):
    features = query.shape[4]
    heads = features // HD
    frames, cols = latent.shape[2], latent.shape[3]
    rows = frames * cols
    bands = lax.axis_size("grp")
    seq_at, grp_at = lax.axis_index("seq"), lax.axis_index("grp")
    videos, tail_frames = frame_tail.shape[0], frame_tail.shape[1]

    sent = pack_heads(
        query.reshape(rows, features),
        key_states.reshape(rows, features),
        value_states.reshape(rows, features),
        heads,
    )
    mine = lax.all_to_all(sent, "seq", 0, 0, tiled=True)

    seq_at, grp_at = seq_at.reshape(1), grp_at.reshape(1)
    lat = jnp.pad(latent.reshape(rows, 4 * LAT_CH), ((0, 0), (SIDE, SIDE)))
    tail = jnp.transpose(frame_tail, (1, 0, 2, 3, 4)).reshape(videos * tail_frames, -1)
    own, above, below = edges(grp_at, tail, lat)

    taps = spread_taps(conv_weight)
    w = lax.dynamic_slice_in_dim(head_weight, seq_at[0] * HD, HD, axis=0)
    w = jnp.concatenate([w[:, SIDE:], w, w[:, :SIDE]], axis=1)
    gain = jnp.tile(latent_scale, HD // LAT_CH).reshape(1, HD)
    shift = jnp.tile(latent_shift, HD // LAT_CH).reshape(1, HD)

    sigma = jnp.broadcast_to(sigma.reshape(1, 1), (1, HD))
    bias = conv_bias.reshape(1, -1)
    mine, w, lat, own, above, below, taps, gain, shift, bias, sigma = lax.optimization_barrier(
        (mine, w, lat, own, above, below, taps, gain, shift, bias, sigma)
    )

    parts = lax.all_to_all(attend(mine, w), "seq", 0, 0, tiled=True)
    bands_out = update(seq_at, parts, lat, above, below, sigma, gain, shift, features, bands)
    tiles = lax.all_to_all(bands_out, "grp", 0, 0, tiled=True)
    return convolve(grp_at, tiles, own, above, below, taps, bias)


def solution(mesh):
    return jax.shard_map(
        on_device,
        mesh=mesh,
        in_specs=(
            P("grp", "seq", None, None, None),
            P("grp", "seq", None, None, None),
            P("grp", "seq", None, None, None),
            P("grp", "seq", None, None, None),
            P("grp"),
            P(),
            P(),
            P(),
            P(None, None, "seq", "grp", None),
            P(),
            P(),
        ),
        out_specs=P(None, None, "seq", "grp", None),
        check_vma=False,
    )
```
